128 devices in a mesh: kpt: 8 (over z, core), row: 4 (over y), col: 4 (over x).
Axes of the slice: x: 4, y: 4, z: 4, core: 2. Of those that a mesh axis runs over, the one named last changes fastest.
Arguments:
- cycle_amplitudes: float32 [16, 2, 1024, 2048], P('kpt', None, 'row', 'col'), may hold values from -6 to 6
- cycle_integrals: float32 [16, 2, 2048, 2048], P('kpt', None, 'row', 'col'), may hold values from -0.09375 to 0.09375
- ladder_weight: float32 [16, 2, 1024, 1024], P('kpt', None, ('row', 'col')), may hold values from -0.125 to 0.125
- momentum_table: int32 [16, 16, 16], replicated, may hold values from 0 to 15, as said below
- transfer_slots: int32 [16], replicated, may hold values from 0 to 15, each once
- momentum_slots: int32 [16], replicated, may hold values from 0 to 15, each once
Outputs:
- residual: float32 [16, 2, 1024, 2048], P('kpt', None, 'row', 'col')
The draws below stay inside these ranges and needn't reach their ends.
Inputs may be any that keep to these rules, and one draw needn't show every extreme that they name: momentum_table[a, b, c] is the label of a + b - c on a periodic grid of 16 k-points; the labels form an abelian group under this addition with label 0 as its anchor. `transfer_slots`: every momentum transfer stands in exactly one slot. `momentum_slots`: every total momentum stands in exactly one slot.
All inputs are finite; a program needn't handle non-finite values.
Results may differ from the reference program's by a relative error of at most 0.00007.
Values sent between devices are 32-bit elements; how exact they have to be, the bound alone decides.
A program may use at most 192 MiB of HBM per device.

```python
import jax
import jax.numpy as jnp
from jax import lax

NK = 16
RP = 64
KP = 128
CP = 128


def draw_momentum_table(key, part):
    shape_key = jax.random.fold_in(key, 11)
    label_key = jax.random.fold_in(key, 12)
    factors = jnp.array([[16, 1, 1], [2, 8, 1], [4, 4, 1], [8, 2, 1], [2, 2, 4], [4, 2, 2]], dtype=jnp.int32)
    shape_pick = jax.random.randint(shape_key, (), 0, 6)
    extents = factors[shape_pick]
    others = jax.random.permutation(label_key, NK - 1).astype(jnp.int32) + 1
    label_of_point = jnp.concatenate([jnp.zeros((1,), jnp.int32), others])
    point_of_label = jnp.argsort(label_of_point).astype(jnp.int32)
    labels = jnp.arange(NK, dtype=jnp.int32)

    def coordinates(points):
        return (points % extents[0], points // extents[0] % extents[1], points // (extents[0] * extents[1]))
    first_coord = coordinates(point_of_label[labels][:, None, None])
    second_coord = coordinates(point_of_label[labels][None, :, None])
    third_coord = coordinates(point_of_label[labels][None, None, :])
    result_coord = [jnp.mod(first_coord[axis_num] + second_coord[axis_num] - third_coord[axis_num], extents[axis_num]) for axis_num in range(3)]
    point = result_coord[0] + extents[0] * (result_coord[1] + extents[1] * result_coord[2])
    return label_of_point[point].astype(jnp.int32)


def level_of(rng, dims, cuts, low, top_value):
    level = 1.0
    for axis_at, blocks in cuts:
        steps = jax.random.uniform(jax.random.fold_in(jax.random.fold_in(rng, 6), axis_at), (blocks,), jnp.float32, low / len(cuts), top_value / len(cuts))
        level = level * jnp.repeat(jnp.exp(steps), dims[axis_at] // blocks).reshape((-1,) + (1,) * (len(dims) - 1 - axis_at))
    return level


def bell_draw(key, extent, spread, reach, shards=(), held_as=jnp.bfloat16):
    loudness = level_of(key, extent, shards, -0.22, 0.18) if shards else 1.0
    drawn = jax.random.normal(key, extent, jnp.float32) * spread * loudness
    return jnp.minimum(jnp.maximum(drawn, -reach), reach).astype(held_as)


def setup_inputs(seed: int = 0) -> dict:
    key_of = jax.random.split(jax.random.key(seed), 7)
    return {
        "cycle_amplitudes": bell_draw(key_of[0], (NK, 2, NK * RP, NK * KP), 1.0, 6.0, ((0, 8), (2, 4), (3, 4)), jnp.float32),
        "cycle_integrals": bell_draw(key_of[1], (NK, 2, NK * KP, NK * CP), (2 * NK * KP) ** -0.5, 0.09375, ((0, 8), (2, 4), (3, 4)), jnp.float32),
        "ladder_weight": bell_draw(key_of[2], (NK, 2, NK * RP, NK * RP), (2 * NK * RP) ** -0.5, 0.125, ((0, 8), (2, 16)), jnp.float32),
        "momentum_table": draw_momentum_table(jax.random.fold_in(key_of[6], 71), 0),
        "transfer_slots": jax.random.permutation(key_of[4], NK).astype(jnp.int32),
        "momentum_slots": jax.random.permutation(key_of[5], NK).astype(jnp.int32),
    }


PRECISE = lax.Precision.HIGHEST


def complex_product(left_op, right_op):
    def multiply(first_mat, second_mat):
        return jnp.dot(first_mat, second_mat, precision=PRECISE, preferred_element_type=jnp.float32)

    real_part = multiply(left_op[0], right_op[0]) - multiply(left_op[1], right_op[1])
    imag_part = multiply(left_op[0], right_op[1]) + multiply(left_op[1], right_op[0])
    return jnp.stack([real_part, imag_part])


def reference(cycle_amplitudes, cycle_integrals, ladder_weight, momentum_table, transfer_slots, momentum_slots):
    labels = jnp.arange(NK, dtype=jnp.int32)
    add_table = momentum_table[:, :, 0]
    sub_table = momentum_table[:, 0, :]
    slot_of_transfer = jnp.argsort(transfer_slots).astype(jnp.int32)
    slot_of_momentum = jnp.argsort(momentum_slots).astype(jnp.int32)
    cycle_out = lax.map(lambda operands: complex_product(operands[0], operands[1]), (cycle_amplitudes, cycle_integrals))
    blocks = cycle_out.reshape(NK, 2, NK, RP, CP, NK).transpose(0, 2, 5, 1, 3, 4)
    pair_sum = add_table[labels[:, None], labels[None, :]]

    def ladder_one(operands):
        weight, momentum = operands
        slot_grid = slot_of_transfer[sub_table[momentum, pair_sum]]
        grouped = blocks[slot_grid, labels[:, None], labels[None, :]]
        grouped = grouped.transpose(2, 0, 3, 4, 1).reshape(2, NK * RP, CP * NK)
        return complex_product(weight, grouped)

    ladder_out = lax.map(ladder_one, (ladder_weight, momentum_slots))
    ladder_blocks = ladder_out.reshape(NK, 2, NK, RP, CP, NK).transpose(0, 2, 5, 1, 3, 4)

    def residual_one(operands):
        cycle_slot, transfer = operands
        shifted = add_table[transfer, labels]
        totals = add_table[shifted[:, None], labels[None, :]]
        slot_grid = slot_of_momentum[totals]
        ladder_part = ladder_blocks[slot_grid, labels[:, None], labels[None, :]]
        ladder_part = ladder_part.transpose(2, 0, 3, 4, 1).reshape(2, NK * RP, CP * NK)
        return cycle_slot + ladder_part

    return lax.map(residual_one, (cycle_out, transfer_slots))
```

```python
import jax
import jax.numpy as jnp
from jax import lax
from jax.experimental import pallas as pl
from jax.experimental.pallas import tpu as pltpu
from jax.sharding import PartitionSpec as P

MESH = pl.DeviceIdType.MESH
F32 = jnp.float32
BF16 = jnp.bfloat16


def split(value):
    high = value.astype(BF16)
    return high, (value - high.astype(F32)).astype(BF16)


def dot3(left, right, dims):
    def dot(a, b):
        return lax.dot_general(a, b, (dims, ((), ())), preferred_element_type=F32)

    return dot(left[0], right[0]) + (dot(left[0], right[1]) + dot(left[1], right[0]))


def exchange_kernel(
    a_in, b_in, w_in, table, transfers, momenta,
    out, out_table,
    a32, b32, w32, bh, bl, c32, ct, cg, gsend, grecv, gt, gh, gl, r32, rsend,
    tg, ts, tk, inv_t, inv_m,
    a_ys, a_yr, a_xs, a_xr, a_fs, a_fr, a_ss, a_sr,
    w_ys, w_yr, w_xs, w_xr, w_fs, w_fr, w_ss, w_sr,
    b_s, b_r, g_s, g_r, r_s, r_r,
):
    k, y, x = lax.axis_index("kpt"), lax.axis_index("row"), lax.axis_index("col")
    z, c = k // 2, lax.rem(k, 2)
    me = 4 * z + y
    left, right, far = lax.rem(x + 3, 4), lax.rem(x + 1, 4), lax.rem(x + 2, 4)
    right_dev, left_dev, twin = (k, y, right), (k, y, left), (2 * z + 1 - c, y, x)

    def rcopy(src, dst, send_sem, recv_sem, dev):
        return pltpu.make_async_remote_copy(
            src_ref=src, dst_ref=dst, send_sem=send_sem, recv_sem=recv_sem,
            device_id=dev, device_id_type=MESH,
        )

    barrier = pltpu.get_barrier_semaphore()

    def greet(at, carry):
        dk, dy = at // 4, lax.rem(at, 4)

        @pl.when(jnp.logical_or(dk != k, dy != y))
        def _():
            pl.semaphore_signal(barrier, inc=1, device_id=(dk, dy, x), device_id_type=MESH)

        return carry

    lax.fori_loop(0, 32, greet, 0)
    pl.semaphore_signal(barrier, inc=1, device_id=right_dev, device_id_type=MESH)
    pl.semaphore_signal(barrier, inc=1, device_id=left_dev, device_id_type=MESH)
    pl.semaphore_wait(barrier, 33)

    def order(n):
        return lax.rem(y + n + (n // 2) * (1 - 2 * lax.rem(n, 2)), 4)

    def row_dest(i, core):
        return (2 * z + core, 2 * c + i, x)

    def is_self(i, core):
        return jnp.logical_and(2 * c + i == y, c == core)

    def start_rows(source, dest, send, recv):
        for i in range(2):
            for core in range(2):
                own = is_self(i, core)

                @pl.when(own)
                def _():
                    pltpu.make_async_copy(source(i, core), dest(core), recv.at[y]).start()

                @pl.when(jnp.logical_not(own))
                def _():
                    rcopy(source(i, core), dest(core), send.at[2 * i + core], recv.at[y], row_dest(i, core)).start()

    def end_rows(source, dest, send, recv):
        for i in range(2):
            for core in range(2):

                @pl.when(jnp.logical_not(is_self(i, core)))
                def _():
                    rcopy(source(i, core), dest(core), send.at[2 * i + core], recv.at[y], row_dest(i, core)).wait_send()

    class Spread:
        def __init__(self, block, rows, sems):
            self.block, self.rows = block, rows
            self.ys, self.yr, self.xs, self.xr, self.fs, self.fr, self.ss, self.sr = sems

        def wait_row(self, m):
            blk = self.block(c, m, x)
            rcopy(blk, blk, self.ys.at[0], self.yr.at[m], twin).wait_recv()

        def across(self, pos, m):
            at = (x, left, right, far)[pos]
            blk = self.block(c, m, at)
            return rcopy(blk, blk, self.ss.at[pos, m], self.sr.at[pos, m], twin)

        def wait_across(self, m):
            for pos, at in enumerate((x, left, right, far)):
                blk = self.block(1 - c, m, at)
                rcopy(blk, blk, self.ss.at[pos, m], self.sr.at[pos, m], twin).wait_recv()

        def step(self, side, m):
            blk = self.block(c, m, x)
            dev = right_dev if side == 0 else left_dev
            return rcopy(blk, blk, self.xs.at[side, m], self.xr.at[side, m], dev)

        def relay(self, side, m):
            blk = self.half(m, left if side == 0 else right, side)
            dev = right_dev if side == 0 else left_dev
            return rcopy(blk, blk, self.fs.at[side, m], self.fr.at[side, m], dev)

        def half(self, m, at, side):
            return self.block(c, m, at).at[pl.ds(side * (self.rows // 2), self.rows // 2)]

        def forward_own(self, m):
            self.step(0, m).start()
            self.step(1, m).start()
            self.across(0, m).start()

        def forward_near(self, m):
            for side, at in ((0, left), (1, right)):
                blk = self.block(c, m, at)
                rcopy(blk, blk, self.xs.at[side, m], self.xr.at[side, m], twin).wait_recv()
                self.relay(side, m).start()
                self.across(1 + side, m).start()

        def forward_far(self, m):
            for side in range(2):
                blk = self.half(m, far, side)
                rcopy(blk, blk, self.fs.at[side, m], self.fr.at[side, m], twin).wait_recv()
            self.across(3, m).start()

        def end(self, m):
            for side in range(2):
                self.step(side, m).wait_send()
                self.relay(side, m).wait_send()
            for pos in range(4):
                self.across(pos, m).wait_send()

    spread_a = Spread(
        lambda core, m, at: a32.at[core, m, at], 256, (a_ys, a_yr, a_xs, a_xr, a_fs, a_fr, a_ss, a_sr)
    )
    spread_w = Spread(
        lambda core, m, at: w32.at[core, 4 * m + at], 64, (w_ys, w_yr, w_xs, w_xr, w_fs, w_fr, w_ss, w_sr)
    )

    a_rows = (lambda i, core: a_in.at[i, core], lambda core: a32.at[core, y, x], a_ys, a_yr)
    w_rows = (lambda i, core: w_in.at[i, core], lambda core: w32.at[core, 4 * y + x], w_ys, w_yr)
    b_rows = (
        lambda i, core: b_in.at[i, :, :, pl.ds(256 * core, 256)], lambda core: b32.at[y], b_s, b_r,
    )
    start_rows(*a_rows)
    spread_a.wait_row(y)
    spread_a.forward_own(y)

    def add(first, second):
        return table[16 * first + second, 0]

    def sub(first, second):
        return table[16 * first, second]

    def invert(label, carry):
        at_t, at_m = 0, 0
        for slot in range(16):
            at_t = jnp.where(transfers[slot] == label, slot, at_t)
            at_m = jnp.where(momenta[slot] == label, slot, at_m)
        inv_t[label] = at_t
        inv_m[label] = at_m
        return carry

    lax.fori_loop(0, 16, invert, 0)
    own_transfer, own_momentum = transfers[me], momenta[me]

    def fill(ki, carry):
        def one(at, inner):
            tg[ki, at] = sub(sub(momenta[at], own_transfer), ki)
            tk[ki, at] = sub(sub(own_momentum, transfers[at]), ki)
            ts[ki, at] = inv_t[sub(sub(own_momentum, ki), at)]
            return inner

        return lax.fori_loop(0, 16, one, carry)

    lax.fori_loop(0, 16, fill, 0)

    def fill_out(at, carry):
        total = add(transfers[2 * k + at // 4], 4 * y + lax.rem(at, 4))

        def one(kb, inner):
            out_table[at, kb] = inv_m[add(total, kb)]
            return inner

        return lax.fori_loop(0, 16, one, carry)

    lax.fori_loop(0, 8, fill_out, 0)

    for n in range(1, 4):
        spread_a.wait_row(order(n))
        spread_a.forward_own(order(n))
    end_rows(*a_rows)
    start_rows(*b_rows)
    for n in range(4):
        spread_a.forward_near(order(n))
    end_rows(*b_rows)
    start_rows(*w_rows)

    for n in range(4):
        at = order(n)
        rcopy(b32.at[at], b32.at[at], b_s.at[0], b_r.at[at], twin).wait_recv()

        def split_b(ri, carry):
            bh[at, ri], bl[at, ri] = split(b32[at, ri])
            return carry

        lax.fori_loop(0, 2, split_b, 0)

    for n in range(4):
        spread_a.forward_far(order(n))

    lower = lax.broadcasted_iota(jnp.int32, (16, 128), 1) < 64

    def pick(load, first, second):
        return jnp.where(lower, load(first), load(second))

    def g_copy(m, slot, source):
        return rcopy(
            gsend.at[m, slot], grecv.at[m, source], g_s.at[m, slot], g_r.at[m, source],
            (2 * (slot // 4) + c, lax.rem(slot, 4), x),
        )

    NN = ((1,), (0,))
    NT = ((1,), (1,))

    def cycle_block(n, carry):
        m = order(n)
        spread_a.wait_across(m)
        c32[...] = jnp.zeros_like(c32)

        def chunk(at, inner):
            a_real, a_imag = split(a32[0, m, at]), split(a32[1, m, at])
            b_real, b_imag = (bh[at, 0], bl[at, 0]), (bh[at, 1], bl[at, 1])
            c32[0] += dot3(a_real, b_real, NN) - dot3(a_imag, b_imag, NN)
            c32[1] += dot3(a_real, b_imag, NN) + dot3(a_imag, b_real, NN)
            return inner

        lax.fori_loop(0, 4, chunk, 0)
        for ri in range(2):
            for h in range(2):
                ct[ri, h] = c32[ri, 128 * h : 128 * h + 128, :].T
                for kb in range(16):
                    cg[ri, kb, :, 128 * h : 128 * h + 128] = ct[ri, h, pl.ds(kb, 16, stride=16), :]

        def to_slot(slot, inner):
            for h in range(2):
                first, second = tg[4 * m + 2 * h, slot], tg[4 * m + 2 * h + 1, slot]
                for ri in range(2):
                    gsend[m, slot, ri, :, 128 * h : 128 * h + 128] = pick(
                        lambda kb: cg[ri, kb, :, pl.ds(128 * h, 128)], first, second
                    )

            @pl.when(slot == me)
            def _():
                pltpu.make_async_copy(gsend.at[m, slot], grecv.at[m, me], g_r.at[m, me]).start()

            @pl.when(slot != me)
            def _():
                g_copy(m, slot, me).start()

            return inner

        lax.fori_loop(0, 16, to_slot, 0)

        @pl.when(n == 1)
        def _():
            for at in range(4):
                spread_w.wait_row(order(at))
                spread_w.forward_own(order(at))

        return carry

    lax.fori_loop(0, 4, cycle_block, 0)

    for n in range(4):
        spread_w.forward_near(order(n))

    def arrive(at, carry):
        slot = at // 4
        g_copy(lax.rem(at, 4), slot, slot).wait_recv()
        return carry

    lax.fori_loop(0, 64, arrive, 0)

    def gather_block(n, carry):
        m = order(n)

        def from_slot(kb, inner):
            for h in range(2):
                first, second = ts[4 * m + 2 * h, kb], ts[4 * m + 2 * h + 1, kb]
                for ri in range(2):
                    gt[ri, m, kb, :, 128 * h : 128 * h + 128] = pick(
                        lambda slot: grecv[m, slot, ri, :, pl.ds(128 * h, 128)], first, second
                    )
            return inner

        lax.fori_loop(0, 16, from_slot, 0)
        for ri in range(2):
            gh[ri, m], gl[ri, m] = split(gt[ri, m].reshape(256, 256))
        return carry

    lax.fori_loop(0, 4, gather_block, 0)

    for n in range(4):
        spread_w.forward_far(order(n))

    def r_copy(m, dest, source):
        return rcopy(rsend.at[m, dest], out.at[source], r_s.at[m, dest], r_r.at[source], (dest, m, x))

    def ladder_block(n, carry):
        m = order(n)
        spread_w.wait_across(m)
        c32[...] = jnp.zeros_like(c32)

        def chunk(at, inner):
            cols = pl.ds(pl.multiple_of(256 * at, 256), 256)
            w_real = split(w32[0, pl.ds(4 * m, 4), :, cols].reshape(256, 256))
            w_imag = split(w32[1, pl.ds(4 * m, 4), :, cols].reshape(256, 256))
            g_real, g_imag = (gh[0, at], gl[0, at]), (gh[1, at], gl[1, at])
            c32[0] += dot3(g_real, w_real, NT) - dot3(g_imag, w_imag, NT)
            c32[1] += dot3(g_imag, w_real, NT) + dot3(g_real, w_imag, NT)
            return inner

        lax.fori_loop(0, 4, chunk, 0)
        for ri in range(2):
            r32[ri] = gt[ri, m] + c32[ri].reshape(16, 16, 256)

        def to_dest(dest, inner):
            for i in range(2):
                for h in range(2):
                    first = tk[4 * m + 2 * h, 2 * dest + i]
                    second = tk[4 * m + 2 * h + 1, 2 * dest + i]
                    for ri in range(2):
                        rsend[m, dest, i, ri, :, 128 * h : 128 * h + 128] = pick(
                            lambda kb: r32[ri, kb, :, pl.ds(128 * h, 128)], first, second
                        )
            own = jnp.logical_and(dest == k, m == y)

            @pl.when(own)
            def _():
                pltpu.make_async_copy(rsend.at[m, dest], out.at[2 * me + c], r_r.at[2 * me + c]).start()

            @pl.when(jnp.logical_not(own))
            def _():
                r_copy(m, dest, 2 * me + c).start()

            return inner

        lax.fori_loop(0, 8, to_dest, 0)
        return carry

    lax.fori_loop(0, 4, ladder_block, 0)

    end_rows(*w_rows)

    def end_block(m, carry):
        spread_a.end(m)
        spread_w.end(m)

        def end_slot(slot, inner):
            @pl.when(slot != me)
            def _():
                g_copy(m, slot, me).wait_send()

            return inner

        lax.fori_loop(0, 16, end_slot, 0)

        def end_dest(dest, inner):
            @pl.when(jnp.logical_or(dest != k, m != y))
            def _():
                r_copy(m, dest, 2 * me + c).wait_send()

            return inner

        return lax.fori_loop(0, 8, end_dest, carry)

    lax.fori_loop(0, 4, end_block, 0)

    def end_source(source, carry):
        r_copy(0, 0, source).wait_recv()
        return carry

    lax.fori_loop(0, 32, end_source, 0)


def place_kernel(slot_of, parts, out, rows):
    at = 4 * pl.program_id(0)
    lower = lax.broadcasted_iota(jnp.int32, (16, 128), 1) < 64
    for h in range(2):

        def one(kb, carry):
            first, second = slot_of[at + 2 * h, kb], slot_of[at + 2 * h + 1, kb]
            for core in range(2):
                value = jnp.where(
                    lower,
                    parts[2 * first + core, 0, 0, :, pl.ds(128 * h, 128)],
                    parts[2 * second + core, 0, 0, :, pl.ds(128 * h, 128)],
                )
                rows[h, pl.ds(256 * core + kb, 16, stride=16), :] = value
            return carry

        lax.fori_loop(0, 16, one, 0)
        out[0, 0, 128 * h : 128 * h + 128, :] = rows[h].T


def body(amplitudes, integrals, weight, table, transfers, momenta):
    dma = pltpu.SemaphoreType.DMA
    spread_sems = [dma((4,)), dma((4,)), dma((2, 4)), dma((2, 4)), dma((2, 4)), dma((2, 4)), dma((4, 4)), dma((4, 4))]
    parts, slot_of = pl.pallas_call(
        exchange_kernel,
        out_shape=(
            jax.ShapeDtypeStruct((32, 2, 2, 16, 256), F32),
            jax.ShapeDtypeStruct((8, 16), jnp.int32),
        ),
        in_specs=[pl.BlockSpec(memory_space=pl.ANY)] * 3 + [pl.BlockSpec(memory_space=pltpu.SMEM)] * 3,
        out_specs=(pl.BlockSpec(memory_space=pl.ANY), pl.BlockSpec(memory_space=pltpu.SMEM)),
        scratch_shapes=[
            pltpu.VMEM((2, 4, 4, 256, 512), F32),
            pltpu.VMEM((4, 2, 512, 256), F32),
            pltpu.VMEM((2, 16, 64, 1024), F32),
            pltpu.VMEM((4, 2, 512, 256), BF16),
            pltpu.VMEM((4, 2, 512, 256), BF16),
            pltpu.VMEM((2, 256, 256), F32),
            pltpu.VMEM((2, 2, 256, 128), F32),
            pltpu.VMEM((2, 16, 16, 256), F32),
            pltpu.VMEM((4, 16, 2, 16, 256), F32),
            pltpu.VMEM((4, 16, 2, 16, 256), F32),
            pltpu.VMEM((2, 4, 16, 16, 256), F32),
            pltpu.VMEM((2, 4, 256, 256), BF16),
            pltpu.VMEM((2, 4, 256, 256), BF16),
            pltpu.VMEM((2, 16, 16, 256), F32),
            pltpu.VMEM((4, 8, 2, 2, 16, 256), F32),
            pltpu.SMEM((16, 16), jnp.int32),
            pltpu.SMEM((16, 16), jnp.int32),
            pltpu.SMEM((16, 16), jnp.int32),
            pltpu.SMEM((16,), jnp.int32),
            pltpu.SMEM((16,), jnp.int32),
        ]
        + spread_sems
        + spread_sems
        + [dma((4,)), dma((4,)), dma((4, 16)), dma((4, 16)), dma((4, 8)), dma((32,))],
        compiler_params=pltpu.CompilerParams(
            collective_id=0, has_side_effects=True, vmem_limit_bytes=60 * 2**20
        ),
        name="exchange",
    )(amplitudes, integrals, weight, table.reshape(256, 16), transfers, momenta)
    return pl.pallas_call(
        place_kernel,
        grid=(2, 2),
        out_shape=jax.ShapeDtypeStruct((2, 2, 256, 512), F32),
        in_specs=[
            pl.BlockSpec(memory_space=pltpu.SMEM),
            pl.BlockSpec((32, 1, 1, 16, 256), lambda i, ri: (0, i, ri, 0, 0)),
        ],
        out_specs=pl.BlockSpec((1, 1, 256, 512), lambda i, ri: (i, ri, 0, 0)),
        scratch_shapes=[pltpu.VMEM((2, 512, 128), F32)],
        name="place",
    )(slot_of, parts)


def solution(mesh):
    return jax.shard_map(
        body,
        mesh=mesh,
        in_specs=(
            P("kpt", None, "row", "col"),
            P("kpt", None, "row", "col"),
            P("kpt", None, ("row", "col"), None),
            P(),
            P(),
            P(),
        ),
        out_specs=P("kpt", None, "row", "col"),
        check_vma=False,
    )
```

```python
import jax
import jax.numpy as jnp
from jax import lax
from jax.experimental import pallas as pl
from jax.experimental.pallas import tpu as pltpu
from jax.sharding import PartitionSpec as P

MESH = pl.DeviceIdType.MESH
F32 = jnp.float32
BF16 = jnp.bfloat16


def split(value):
    high = value.astype(BF16)
    return high, (value - high.astype(F32)).astype(BF16)


def dot3(left, right, dims):
    def dot(a, b):
        return lax.dot_general(a, b, (dims, ((), ())), preferred_element_type=F32)

    return dot(left[0], right[0]) + (dot(left[0], right[1]) + dot(left[1], right[0]))


def exchange_kernel(
    a_in, b_in, w_in, table_in, transfers_in, momenta_in,
    out, out_table,
    a32, b32, w32, bh, bl, c32, ct, cg, gsend, grecv, gt, gh, gl, r32, rsend,
    table, transfers, momenta, tg, ts, tk, inv_t, inv_m, table_sem,
    a_ys, a_yr, a_xs, a_xr, a_fs, a_fr, a_ss, a_sr,
    w_ys, w_yr, w_xs, w_xr, w_fs, w_fr, w_ss, w_sr,
    b_s, b_r, g_s, g_r, r_s, r_r,
):
    k, y, x = lax.axis_index("kpt"), lax.axis_index("row"), lax.axis_index("col")
    z, c = k // 2, lax.rem(k, 2)
    me = 4 * z + y
    left, right, far = lax.rem(x + 3, 4), lax.rem(x + 1, 4), lax.rem(x + 2, 4)
    right_dev, left_dev, twin = (k, y, right), (k, y, left), (2 * z + 1 - c, y, x)

    def rcopy(src, dst, send_sem, recv_sem, dev):
        return pltpu.make_async_remote_copy(
            src_ref=src, dst_ref=dst, send_sem=send_sem, recv_sem=recv_sem,
            device_id=dev, device_id_type=MESH,
        )

    barrier = pltpu.get_barrier_semaphore()

    for step in range(1, 32):
        dk = 2 * lax.rem(z + step // 8, 4) + lax.rem(c + step // 4 % 2, 2)
        pl.semaphore_signal(
            barrier, inc=1, device_id=(dk, lax.rem(y + step % 4, 4), x), device_id_type=MESH
        )
    pl.semaphore_signal(barrier, inc=1, device_id=right_dev, device_id_type=MESH)
    pl.semaphore_signal(barrier, inc=1, device_id=left_dev, device_id_type=MESH)
    pl.semaphore_wait(barrier, 33)

    def order(n):
        return lax.rem(y + n + (n // 2) * (1 - 2 * lax.rem(n, 2)), 4)

    def far_order(n):
        return lax.rem(y + 2 + 3 * n, 4)

    near_i, other_i = 1 - lax.rem(y, 2), lax.rem(y, 2)
    home = c == y // 2

    class Rows:
        def __init__(self, source, dest, send, recv):
            self.source, self.dest, self.send, self.recv = source, dest, send, recv

        def copy(self, near, core):
            i = near_i if near else other_i
            return rcopy(
                self.source(i, core), self.dest(core), self.send.at[core if near else 2 + core],
                self.recv.at[y], (2 * z + core, 2 * c + i, x),
            )

        def start_near(self):
            for core in range(2):
                self.copy(True, core).start()

        def start_home(self):
            for core in range(2):

                @pl.when(jnp.logical_and(home, c == core))
                def _():
                    pltpu.make_async_copy(self.source(other_i, core), self.dest(core), self.recv.at[y]).start()

                @pl.when(jnp.logical_and(home, c != core))
                def _():
                    self.copy(False, core).start()

        def start_far(self):
            for core in range(2):

                @pl.when(jnp.logical_not(home))
                def _():
                    self.copy(False, core).start()

        def end_near(self):
            for core in range(2):
                self.copy(True, core).wait_send()

        def end_other(self):
            for core in range(2):

                @pl.when(jnp.logical_not(jnp.logical_and(home, c == core)))
                def _():
                    self.copy(False, core).wait_send()

    class Spread:
        def __init__(self, block, rows, sems):
            self.block, self.rows = block, rows
            self.ys, self.yr, self.xs, self.xr, self.fs, self.fr, self.ss, self.sr = sems

        def wait_row(self, m):
            blk = self.block(c, m, x)
            rcopy(blk, blk, self.ys.at[0], self.yr.at[m], twin).wait_recv()

        def across(self, pos, m):
            at = (x, left, right, far)[pos]
            blk = self.block(c, m, at)
            return rcopy(blk, blk, self.ss.at[pos, m], self.sr.at[pos, m], twin)

        def wait_across(self, m):
            for pos, at in enumerate((x, left, right, far)):
                blk = self.block(1 - c, m, at)
                rcopy(blk, blk, self.ss.at[pos, m], self.sr.at[pos, m], twin).wait_recv()

        def step(self, side, m):
            blk = self.block(c, m, x)
            dev = right_dev if side == 0 else left_dev
            return rcopy(blk, blk, self.xs.at[side, m], self.xr.at[side, m], dev)

        def relay(self, side, m):
            blk = self.half(m, left if side == 0 else right, side)
            dev = right_dev if side == 0 else left_dev
            return rcopy(blk, blk, self.fs.at[side, m], self.fr.at[side, m], dev)

        def half(self, m, at, side):
            return self.block(c, m, at).at[pl.ds(side * (self.rows // 2), self.rows // 2)]

        def forward_own(self, m):
            self.step(0, m).start()
            self.step(1, m).start()
            self.across(0, m).start()

        def forward_near(self, m):
            for side, at in ((0, left), (1, right)):
                blk = self.block(c, m, at)
                rcopy(blk, blk, self.xs.at[side, m], self.xr.at[side, m], twin).wait_recv()
                self.relay(side, m).start()
                self.across(1 + side, m).start()

        def forward_far(self, m):
            for side in range(2):
                blk = self.half(m, far, side)
                rcopy(blk, blk, self.fs.at[side, m], self.fr.at[side, m], twin).wait_recv()
            self.across(3, m).start()

        def end(self, m):
            for side in range(2):
                self.step(side, m).wait_send()
                self.relay(side, m).wait_send()
            for pos in range(4):
                self.across(pos, m).wait_send()

    spread_a = Spread(
        lambda core, m, at: a32.at[core, m, at], 256, (a_ys, a_yr, a_xs, a_xr, a_fs, a_fr, a_ss, a_sr)
    )
    spread_w = Spread(
        lambda core, m, at: w32.at[core, 4 * m + at], 64, (w_ys, w_yr, w_xs, w_xr, w_fs, w_fr, w_ss, w_sr)
    )

    a_rows = Rows(lambda i, core: a_in.at[i, core], lambda core: a32.at[core, y, x], a_ys, a_yr)
    w_rows = Rows(lambda i, core: w_in.at[i, core], lambda core: w32.at[core, 4 * y + x], w_ys, w_yr)
    b_rows = Rows(lambda i, core: b_in.at[i, :, :, pl.ds(256 * core, 256)], lambda core: b32.at[y], b_s, b_r)
    for rows in (a_rows, b_rows, w_rows):
        rows.start_home()
    a_rows.start_near()
    a_rows.start_far()
    b_rows.start_near()
    w_rows.start_near()
    w_rows.start_far()
    b_rows.start_far()
    spread_a.wait_row(y)
    spread_a.forward_own(y)

    tables = [
        pltpu.make_async_copy(source, dest, table_sem.at[at])
        for at, (source, dest) in enumerate(
            ((table_in, table), (transfers_in, transfers), (momenta_in, momenta))
        )
    ]
    for copy in tables:
        copy.start()
    for copy in tables:
        copy.wait()

    def add(first, second):
        return table[16 * first + second, 0]

    def sub(first, second):
        return table[16 * first, second]

    def invert(label, carry):
        at_t, at_m = 0, 0
        for slot in range(16):
            at_t = jnp.where(transfers[slot] == label, slot, at_t)
            at_m = jnp.where(momenta[slot] == label, slot, at_m)
        inv_t[label] = at_t
        inv_m[label] = at_m
        return carry

    lax.fori_loop(0, 16, invert, 0)
    own_transfer, own_momentum = transfers[me], momenta[me]

    def fill(ki, carry):
        def one(at, inner):
            tg[ki, at] = sub(sub(momenta[at], own_transfer), ki)
            tk[ki, at] = sub(sub(own_momentum, transfers[at]), ki)
            ts[ki, at] = inv_t[sub(sub(own_momentum, ki), at)]
            return inner

        return lax.fori_loop(0, 16, one, carry)

    lax.fori_loop(0, 16, fill, 0)

    def fill_out(at, carry):
        total = add(transfers[2 * k + at // 4], 4 * y + lax.rem(at, 4))

        def one(kb, inner):
            out_table[at, kb] = inv_m[add(total, kb)]
            return inner

        return lax.fori_loop(0, 16, one, carry)

    lax.fori_loop(0, 8, fill_out, 0)

    def split_b(n):
        at = order(n)
        rcopy(b32.at[at], b32.at[at], b_s.at[0], b_r.at[at], twin).wait_recv()

        def one(ri, carry):
            bh[at, ri], bl[at, ri] = split(b32[at, ri])
            return carry

        lax.fori_loop(0, 2, one, 0)

    NN = ((1,), (0,))
    NT = ((1,), (1,))

    def cycle_chunk(m, at):
        a_real, a_imag = split(a32[0, m, at]), split(a32[1, m, at])
        b_real, b_imag = (bh[at, 0], bl[at, 0]), (bh[at, 1], bl[at, 1])
        c32[m, 0] += dot3(a_real, b_real, NN) - dot3(a_imag, b_imag, NN)
        c32[m, 1] += dot3(a_real, b_imag, NN) + dot3(a_imag, b_real, NN)

    def early_chunks(n):
        m = order(n)
        spread_a.wait_across(m)

        def one(at, carry):
            cycle_chunk(m, order(at))
            return carry

        lax.fori_loop(0, 3, one, 0)

    c32[...] = jnp.zeros_like(c32)
    for n in (1, 2, 3):
        spread_a.wait_row(order(n))
        spread_a.forward_own(order(n))
        if n < 3:
            spread_a.forward_near(order(n - 1))
    split_b(0)
    spread_a.forward_far(y)
    spread_a.forward_near(order(2))
    split_b(1)
    split_b(2)
    early_chunks(0)
    spread_a.forward_far(order(1))
    early_chunks(1)
    spread_a.forward_near(order(3))
    for n in range(4):
        spread_w.wait_row(far_order(n))
        spread_w.forward_own(far_order(n))
    spread_a.forward_far(order(2))
    early_chunks(2)
    spread_a.forward_far(order(3))
    early_chunks(3)
    split_b(3)

    lower = lax.broadcasted_iota(jnp.int32, (16, 128), 1) < 64

    def pick(load, first, second):
        return jnp.where(lower, load(first), load(second))

    def g_copy(m, slot, source):
        return rcopy(
            gsend.at[m, slot], grecv.at[m, source], g_s.at[m, slot], g_r.at[m, source],
            (2 * (slot // 4) + c, lax.rem(slot, 4), x),
        )

    def cycle_block(n, carry):
        m = order(n)
        cycle_chunk(m, order(3))
        for ri in range(2):
            for h in range(2):
                ct[ri, h] = c32[m, ri, 128 * h : 128 * h + 128, :].T
                for kb in range(16):
                    cg[ri, kb, :, 128 * h : 128 * h + 128] = ct[ri, h, pl.ds(kb, 16, stride=16), :]

        def to_slot(step, inner):
            slot_z, slot_y = lax.rem(z + 2 + 3 * (step // 4), 4), lax.rem(y + 2 + 3 * lax.rem(step, 4), 4)
            slot = 4 * slot_z + slot_y
            for h in range(2):
                first, second = tg[4 * m + 2 * h, slot], tg[4 * m + 2 * h + 1, slot]
                for ri in range(2):
                    gsend[m, slot, ri, :, 128 * h : 128 * h + 128] = pick(
                        lambda kb: cg[ri, kb, :, pl.ds(128 * h, 128)], first, second
                    )

            @pl.when(slot == me)
            def _():
                pltpu.make_async_copy(gsend.at[m, slot], grecv.at[m, me], g_r.at[m, me]).start()

            @pl.when(slot != me)
            def _():
                g_copy(m, slot, me).start()

            return inner

        lax.fori_loop(0, 16, to_slot, 0)
        return carry

    lax.fori_loop(0, 4, cycle_block, 0)
    for n in range(4):
        spread_w.forward_near(far_order(n))
    for n in (0, 1):
        spread_w.forward_far(far_order(n))

    def arrive(at, carry):
        slot = at // 4
        g_copy(lax.rem(at, 4), slot, slot).wait_recv()
        return carry

    lax.fori_loop(0, 64, arrive, 0)

    def gather_block(n, carry):
        m = order(n)

        def from_slot(kb, inner):
            for h in range(2):
                first, second = ts[4 * m + 2 * h, kb], ts[4 * m + 2 * h + 1, kb]
                for ri in range(2):
                    gt[ri, m, kb, :, 128 * h : 128 * h + 128] = pick(
                        lambda slot: grecv[m, slot, ri, :, pl.ds(128 * h, 128)], first, second
                    )
            return inner

        lax.fori_loop(0, 16, from_slot, 0)
        for ri in range(2):
            gh[ri, m], gl[ri, m] = split(gt[ri, m].reshape(256, 256))
        return carry

    lax.fori_loop(0, 4, gather_block, 0)

    def r_copy(m, dest, source):
        return rcopy(rsend.at[m, dest], out.at[source], r_s.at[m, dest], r_r.at[source], (dest, m, x))

    def ladder_block(n, carry):
        m = far_order(n)

        @pl.when(n < 2)
        def _():
            spread_w.forward_far(far_order(n + 2))

        spread_w.wait_across(m)
        c32[0] = jnp.zeros_like(c32[0])

        def chunk(at, inner):
            cols = pl.ds(pl.multiple_of(256 * at, 256), 256)
            w_real = split(w32[0, pl.ds(4 * m, 4), :, cols].reshape(256, 256))
            w_imag = split(w32[1, pl.ds(4 * m, 4), :, cols].reshape(256, 256))
            g_real, g_imag = (gh[0, at], gl[0, at]), (gh[1, at], gl[1, at])
            c32[0, 0] += dot3(g_real, w_real, NT) - dot3(g_imag, w_imag, NT)
            c32[0, 1] += dot3(g_imag, w_real, NT) + dot3(g_real, w_imag, NT)
            return inner

        lax.fori_loop(0, 4, chunk, 0)
        for ri in range(2):
            r32[ri] = gt[ri, m] + c32[0, ri].reshape(16, 16, 256)

        def to_dest(step, inner):
            dest = 2 * lax.rem(z + 2 + 3 * (step // 2), 4) + lax.rem(step, 2)
            for i in range(2):
                for h in range(2):
                    first = tk[4 * m + 2 * h, 2 * dest + i]
                    second = tk[4 * m + 2 * h + 1, 2 * dest + i]
                    for ri in range(2):
                        rsend[m, dest, i, ri, :, 128 * h : 128 * h + 128] = pick(
                            lambda kb: r32[ri, kb, :, pl.ds(128 * h, 128)], first, second
                        )
            own = jnp.logical_and(dest == k, m == y)

            @pl.when(own)
            def _():
                pltpu.make_async_copy(rsend.at[m, dest], out.at[2 * me + c], r_r.at[2 * me + c]).start()

            @pl.when(jnp.logical_not(own))
            def _():
                r_copy(m, dest, 2 * me + c).start()

            return inner

        lax.fori_loop(0, 8, to_dest, 0)
        return carry

    lax.fori_loop(0, 4, ladder_block, 0)

    for rows in (a_rows, b_rows, w_rows):
        rows.end_near()
        rows.end_other()

    def end_block(m, carry):
        spread_a.end(m)
        spread_w.end(m)

        def end_slot(slot, inner):
            @pl.when(slot != me)
            def _():
                g_copy(m, slot, me).wait_send()

            return inner

        lax.fori_loop(0, 16, end_slot, 0)

        def end_dest(dest, inner):
            @pl.when(jnp.logical_or(dest != k, m != y))
            def _():
                r_copy(m, dest, 2 * me + c).wait_send()

            return inner

        return lax.fori_loop(0, 8, end_dest, carry)

    lax.fori_loop(0, 4, end_block, 0)

    def end_source(source, carry):
        r_copy(0, 0, source).wait_recv()
        return carry

    lax.fori_loop(0, 32, end_source, 0)


def place_kernel(slot_of, parts, out, rows):
    at = 4 * pl.program_id(0)
    lower = lax.broadcasted_iota(jnp.int32, (16, 128), 1) < 64
    for h in range(2):

        def one(kb, carry):
            first, second = slot_of[at + 2 * h, kb], slot_of[at + 2 * h + 1, kb]
            for core in range(2):
                value = jnp.where(
                    lower,
                    parts[2 * first + core, 0, 0, :, pl.ds(128 * h, 128)],
                    parts[2 * second + core, 0, 0, :, pl.ds(128 * h, 128)],
                )
                rows[h, pl.ds(256 * core + kb, 16, stride=16), :] = value
            return carry

        lax.fori_loop(0, 16, one, 0, unroll=True)
        out[0, 0, 128 * h : 128 * h + 128, :] = rows[h].T


def body(amplitudes, integrals, weight, table, transfers, momenta):
    dma = pltpu.SemaphoreType.DMA
    spread_sems = [dma((4,)), dma((4,)), dma((2, 4)), dma((2, 4)), dma((2, 4)), dma((2, 4)), dma((4, 4)), dma((4, 4))]
    parts, slot_of = pl.pallas_call(
        exchange_kernel,
        out_shape=(
            jax.ShapeDtypeStruct((32, 2, 2, 16, 256), F32),
            jax.ShapeDtypeStruct((8, 16), jnp.int32),
        ),
        in_specs=[pl.BlockSpec(memory_space=pl.ANY)] * 6,
        out_specs=(pl.BlockSpec(memory_space=pl.ANY), pl.BlockSpec(memory_space=pltpu.SMEM)),
        scratch_shapes=[
            pltpu.VMEM((2, 4, 4, 256, 512), F32),
            pltpu.VMEM((4, 2, 512, 256), F32),
            pltpu.VMEM((2, 16, 64, 1024), F32),
            pltpu.VMEM((4, 2, 512, 256), BF16),
            pltpu.VMEM((4, 2, 512, 256), BF16),
            pltpu.VMEM((4, 2, 256, 256), F32),
            pltpu.VMEM((2, 2, 256, 128), F32),
            pltpu.VMEM((2, 16, 16, 256), F32),
            pltpu.VMEM((4, 16, 2, 16, 256), F32),
            pltpu.VMEM((4, 16, 2, 16, 256), F32),
            pltpu.VMEM((2, 4, 16, 16, 256), F32),
            pltpu.VMEM((2, 4, 256, 256), BF16),
            pltpu.VMEM((2, 4, 256, 256), BF16),
            pltpu.VMEM((2, 16, 16, 256), F32),
            pltpu.VMEM((4, 8, 2, 2, 16, 256), F32),
            pltpu.SMEM((256, 16), jnp.int32),
            pltpu.SMEM((16,), jnp.int32),
            pltpu.SMEM((16,), jnp.int32),
            pltpu.SMEM((16, 16), jnp.int32),
            pltpu.SMEM((16, 16), jnp.int32),
            pltpu.SMEM((16, 16), jnp.int32),
            pltpu.SMEM((16,), jnp.int32),
            pltpu.SMEM((16,), jnp.int32),
            dma((3,)),
        ]
        + spread_sems
        + spread_sems
        + [dma((4,)), dma((4,)), dma((4, 16)), dma((4, 16)), dma((4, 8)), dma((32,))],
        compiler_params=pltpu.CompilerParams(
            collective_id=0, has_side_effects=True, vmem_limit_bytes=60 * 2**20
        ),
        name="exchange",
    )(amplitudes, integrals, weight, table.reshape(256, 16), transfers, momenta)
    return pl.pallas_call(
        place_kernel,
        grid=(2, 2),
        out_shape=jax.ShapeDtypeStruct((2, 2, 256, 512), F32),
        in_specs=[
            pl.BlockSpec(memory_space=pltpu.SMEM),
            pl.BlockSpec((32, 1, 1, 16, 256), lambda i, ri: (0, i, ri, 0, 0)),
        ],
        out_specs=pl.BlockSpec((1, 1, 256, 512), lambda i, ri: (i, ri, 0, 0)),
        scratch_shapes=[pltpu.VMEM((2, 512, 128), F32)],
        name="place",
    )(slot_of, parts)


def solution(mesh):
    return jax.shard_map(
        body,
        mesh=mesh,
        in_specs=(
            P("kpt", None, "row", "col"),
            P("kpt", None, "row", "col"),
            P("kpt", None, ("row", "col"), None),
            P(),
            P(),
            P(),
        ),
        out_specs=P("kpt", None, "row", "col"),
        check_vma=False,
    )
```

```python
import jax
import jax.numpy as jnp
from jax import lax
from jax.experimental import pallas as pl
from jax.experimental.pallas import tpu as pltpu
from jax.sharding import PartitionSpec as P

MESH = pl.DeviceIdType.MESH
F32 = jnp.float32
BF16 = jnp.bfloat16


def split(value):
    high = value.astype(BF16)
    return high, (value - high.astype(F32)).astype(BF16)


def dot3(left, right, dims):
    def dot(a, b):
        return lax.dot_general(a, b, (dims, ((), ())), preferred_element_type=F32)

    return dot(left[0], right[0]) + (dot(left[0], right[1]) + dot(left[1], right[0]))


def exchange_kernel(
    a_in, b_in, w_in, table_in, transfers_in, momenta_in,
    out, out_table,
    a32, b32, w32, bh, bl, c32, ct, cg, gsend, grecv, gt, gh, gl, r32, rsend,
    table, transfers, momenta, tg, ts, tk, inv_t, inv_m, table_sem,
    a_ys, a_yr, a_xs, a_xr, a_fs, a_fr, a_ss, a_sr,
    w_ys, w_yr, w_xs, w_xr, w_fs, w_fr, w_ss, w_sr,
    b_s, b_r, g_s, g_r, r_s, r_r,
):
    k, y, x = lax.axis_index("kpt"), lax.axis_index("row"), lax.axis_index("col")
    z, c = k // 2, lax.rem(k, 2)
    me = 4 * z + y
    left, right, far = lax.rem(x + 3, 4), lax.rem(x + 1, 4), lax.rem(x + 2, 4)
    right_dev, left_dev, twin = (k, y, right), (k, y, left), (2 * z + 1 - c, y, x)

    def rcopy(src, dst, send_sem, recv_sem, dev):
        return pltpu.make_async_remote_copy(
            src_ref=src, dst_ref=dst, send_sem=send_sem, recv_sem=recv_sem,
            device_id=dev, device_id_type=MESH,
        )

    barrier = pltpu.get_barrier_semaphore()

    for step in range(1, 32):
        dk = 2 * lax.rem(z + step // 8, 4) + lax.rem(c + step // 4 % 2, 2)
        pl.semaphore_signal(
            barrier, inc=1, device_id=(dk, lax.rem(y + step % 4, 4), x), device_id_type=MESH
        )
    pl.semaphore_signal(barrier, inc=1, device_id=right_dev, device_id_type=MESH)
    pl.semaphore_signal(barrier, inc=1, device_id=left_dev, device_id_type=MESH)
    pl.semaphore_wait(barrier, 33)

    def order(n):
        return lax.rem(y + n + (n // 2) * (1 - 2 * lax.rem(n, 2)), 4)

    def far_order(n):
        return lax.rem(y + 2 + 3 * n, 4)

    near_i, other_i = 1 - lax.rem(y, 2), lax.rem(y, 2)
    home = c == y // 2

    class Rows:
        def __init__(self, source, dest, send, recv):
            self.source, self.dest, self.send, self.recv = source, dest, send, recv

        def copy(self, near, core):
            i = near_i if near else other_i
            return rcopy(
                self.source(i, core), self.dest(core), self.send.at[core if near else 2 + core],
                self.recv.at[y], (2 * z + core, 2 * c + i, x),
            )

        def start_near(self):
            for core in range(2):
                self.copy(True, core).start()

        def start_home(self):
            for core in range(2):

                @pl.when(jnp.logical_and(home, c == core))
                def _():
                    pltpu.make_async_copy(self.source(other_i, core), self.dest(core), self.recv.at[y]).start()

                @pl.when(jnp.logical_and(home, c != core))
                def _():
                    self.copy(False, core).start()

        def start_far(self):
            for core in range(2):

                @pl.when(jnp.logical_not(home))
                def _():
                    self.copy(False, core).start()

        def end_near(self):
            for core in range(2):
                self.copy(True, core).wait_send()

        def end_other(self):
            for core in range(2):

                @pl.when(jnp.logical_not(jnp.logical_and(home, c == core)))
                def _():
                    self.copy(False, core).wait_send()

    class Spread:
        def __init__(self, block, rows, sems):
            self.block, self.rows = block, rows
            self.ys, self.yr, self.xs, self.xr, self.fs, self.fr, self.ss, self.sr = sems

        def wait_row(self, m):
            blk = self.block(c, m, x)
            rcopy(blk, blk, self.ys.at[0], self.yr.at[m], twin).wait_recv()

        def across(self, pos, m):
            at = (x, left, right, far)[pos]
            blk = self.block(c, m, at)
            return rcopy(blk, blk, self.ss.at[pos, m], self.sr.at[pos, m], twin)

        def wait_across(self, m):
            for pos, at in enumerate((x, left, right, far)):
                blk = self.block(1 - c, m, at)
                rcopy(blk, blk, self.ss.at[pos, m], self.sr.at[pos, m], twin).wait_recv()

        def step(self, side, m):
            blk = self.block(c, m, x)
            dev = right_dev if side == 0 else left_dev
            return rcopy(blk, blk, self.xs.at[side, m], self.xr.at[side, m], dev)

        def relay(self, side, m):
            blk = self.half(m, left if side == 0 else right, side)
            dev = right_dev if side == 0 else left_dev
            return rcopy(blk, blk, self.fs.at[side, m], self.fr.at[side, m], dev)

        def half(self, m, at, side):
            return self.block(c, m, at).at[pl.ds(side * (self.rows // 2), self.rows // 2)]

        def forward_own(self, m):
            self.step(0, m).start()
            self.step(1, m).start()
            self.across(0, m).start()

        def forward_near(self, m):
            for side, at in ((0, left), (1, right)):
                blk = self.block(c, m, at)
                rcopy(blk, blk, self.xs.at[side, m], self.xr.at[side, m], twin).wait_recv()
                self.relay(side, m).start()
                self.across(1 + side, m).start()

        def forward_far(self, m):
            for side in range(2):
                blk = self.half(m, far, side)
                rcopy(blk, blk, self.fs.at[side, m], self.fr.at[side, m], twin).wait_recv()
            self.across(3, m).start()

        def end(self, m):
            for side in range(2):
                self.step(side, m).wait_send()
                self.relay(side, m).wait_send()
            for pos in range(4):
                self.across(pos, m).wait_send()

    spread_a = Spread(
        lambda core, m, at: a32.at[core, m, at], 256, (a_ys, a_yr, a_xs, a_xr, a_fs, a_fr, a_ss, a_sr)
    )
    spread_w = Spread(
        lambda core, m, at: w32.at[core, 4 * m + at], 64, (w_ys, w_yr, w_xs, w_xr, w_fs, w_fr, w_ss, w_sr)
    )

    a_rows = Rows(lambda i, core: a_in.at[i, core], lambda core: a32.at[core, y, x], a_ys, a_yr)
    w_rows = Rows(lambda i, core: w_in.at[i, core], lambda core: w32.at[core, 4 * y + x], w_ys, w_yr)
    b_rows = Rows(lambda i, core: b_in.at[i, :, :, pl.ds(256 * core, 256)], lambda core: b32.at[y], b_s, b_r)
    for rows in (a_rows, b_rows, w_rows):
        rows.start_home()
    a_rows.start_near()
    a_rows.start_far()
    b_rows.start_near()
    w_rows.start_near()
    w_rows.start_far()
    b_rows.start_far()
    spread_a.wait_row(y)
    spread_a.forward_own(y)

    tables = [
        pltpu.make_async_copy(source, dest, table_sem.at[at])
        for at, (source, dest) in enumerate(
            ((table_in, table), (transfers_in, transfers), (momenta_in, momenta))
        )
    ]
    for copy in tables:
        copy.start()
    for copy in tables:
        copy.wait()

    def add(first, second):
        return table[16 * first + second, 0]

    def sub(first, second):
        return table[16 * first, second]

    def invert(label, carry):
        at_t, at_m = 0, 0
        for slot in range(16):
            at_t = jnp.where(transfers[slot] == label, slot, at_t)
            at_m = jnp.where(momenta[slot] == label, slot, at_m)
        inv_t[label] = at_t
        inv_m[label] = at_m
        return carry

    lax.fori_loop(0, 16, invert, 0)
    own_transfer, own_momentum = transfers[me], momenta[me]

    def fill(ki, carry):
        def one(at, inner):
            tg[ki, at] = sub(sub(momenta[at], own_transfer), ki)
            tk[ki, at] = sub(sub(own_momentum, transfers[at]), ki)
            ts[ki, at] = inv_t[sub(sub(own_momentum, ki), at)]
            return inner

        return lax.fori_loop(0, 16, one, carry)

    lax.fori_loop(0, 16, fill, 0)

    def fill_out(at, carry):
        total = add(transfers[2 * k + at // 4], 4 * y + lax.rem(at, 4))

        def one(kb, inner):
            out_table[at, kb] = inv_m[add(total, kb)]
            return inner

        return lax.fori_loop(0, 16, one, carry)

    lax.fori_loop(0, 8, fill_out, 0)

    def split_b(n):
        at = order(n)
        rcopy(b32.at[at], b32.at[at], b_s.at[0], b_r.at[at], twin).wait_recv()

        def one(ri, carry):
            bh[at, ri], bl[at, ri] = split(b32[at, ri])
            return carry

        lax.fori_loop(0, 2, one, 0)

    NN = ((1,), (0,))
    NT = ((1,), (1,))

    def cycle_chunk(m, at):
        a_real, a_imag = split(a32[0, m, at]), split(a32[1, m, at])
        b_real, b_imag = (bh[at, 0], bl[at, 0]), (bh[at, 1], bl[at, 1])
        c32[m, 0] += dot3(a_real, b_real, NN) - dot3(a_imag, b_imag, NN)
        c32[m, 1] += dot3(a_real, b_imag, NN) + dot3(a_imag, b_real, NN)

    def early_chunks(n):
        m = order(n)
        spread_a.wait_across(m)

        def one(at, carry):
            cycle_chunk(m, order(at))
            return carry

        lax.fori_loop(0, 3, one, 0)

    c32[...] = jnp.zeros_like(c32)
    for n in (1, 2, 3):
        spread_a.wait_row(order(n))
        spread_a.forward_own(order(n))
        if n < 3:
            spread_a.forward_near(order(n - 1))
    split_b(0)
    spread_a.forward_far(y)
    spread_a.forward_near(order(2))
    spread_a.forward_far(order(1))
    spread_a.forward_near(order(3))
    split_b(1)
    split_b(2)
    early_chunks(0)
    spread_a.forward_far(order(2))
    early_chunks(1)
    spread_a.forward_far(order(3))
    for n in range(4):
        spread_w.wait_row(far_order(n))
        spread_w.forward_own(far_order(n))
    early_chunks(2)
    early_chunks(3)
    split_b(3)

    lower = lax.broadcasted_iota(jnp.int32, (16, 128), 1) < 64

    def pick(load, first, second):
        return jnp.where(lower, load(first), load(second))

    def g_copy(m, slot, source):
        return rcopy(
            gsend.at[m, slot], grecv.at[m, source], g_s.at[m, slot], g_r.at[m, source],
            (2 * (slot // 4) + c, lax.rem(slot, 4), x),
        )

    def cycle_block(n, carry):
        m = order(n)
        cycle_chunk(m, order(3))
        for ri in range(2):
            for h in range(2):
                ct[ri, h] = c32[m, ri, 128 * h : 128 * h + 128, :].T
                for kb in range(16):
                    cg[ri, kb, :, 128 * h : 128 * h + 128] = ct[ri, h, pl.ds(kb, 16, stride=16), :]

        def to_slot(step, inner):
            slot_z, slot_y = lax.rem(z + 2 + 3 * (step // 4), 4), lax.rem(y + 2 + 3 * lax.rem(step, 4), 4)
            slot = 4 * slot_z + slot_y
            for h in range(2):
                first, second = tg[4 * m + 2 * h, slot], tg[4 * m + 2 * h + 1, slot]
                for ri in range(2):
                    gsend[m, slot, ri, :, 128 * h : 128 * h + 128] = pick(
                        lambda kb: cg[ri, kb, :, pl.ds(128 * h, 128)], first, second
                    )

            @pl.when(slot == me)
            def _():
                pltpu.make_async_copy(gsend.at[m, slot], grecv.at[m, me], g_r.at[m, me]).start()

            @pl.when(slot != me)
            def _():
                g_copy(m, slot, me).start()

            return inner

        lax.fori_loop(0, 16, to_slot, 0)
        return carry

    lax.fori_loop(0, 4, cycle_block, 0)
    for n in range(4):
        spread_w.forward_near(far_order(n))
    for n in (0, 1):
        spread_w.forward_far(far_order(n))

    def arrive(at, carry):
        slot = at // 4
        g_copy(lax.rem(at, 4), slot, slot).wait_recv()
        return carry

    lax.fori_loop(0, 64, arrive, 0)

    def gather_block(n, carry):
        m = order(n)

        def from_slot(kb, inner):
            for h in range(2):
                first, second = ts[4 * m + 2 * h, kb], ts[4 * m + 2 * h + 1, kb]
                for ri in range(2):
                    gt[ri, m, kb, :, 128 * h : 128 * h + 128] = pick(
                        lambda slot: grecv[m, slot, ri, :, pl.ds(128 * h, 128)], first, second
                    )
            return inner

        lax.fori_loop(0, 16, from_slot, 0)
        for ri in range(2):
            gh[ri, m], gl[ri, m] = split(gt[ri, m].reshape(256, 256))
        return carry

    lax.fori_loop(0, 4, gather_block, 0)

    def r_copy(m, dest, source):
        return rcopy(rsend.at[m, dest], out.at[source], r_s.at[m, dest], r_r.at[source], (dest, m, x))

    def ladder_block(n, carry):
        m = far_order(n)

        @pl.when(n < 2)
        def _():
            spread_w.forward_far(far_order(n + 2))

        spread_w.wait_across(m)
        c32[0] = jnp.zeros_like(c32[0])

        def chunk(at, inner):
            cols = pl.ds(pl.multiple_of(256 * at, 256), 256)
            w_real = split(w32[0, pl.ds(4 * m, 4), :, cols].reshape(256, 256))
            w_imag = split(w32[1, pl.ds(4 * m, 4), :, cols].reshape(256, 256))
            g_real, g_imag = (gh[0, at], gl[0, at]), (gh[1, at], gl[1, at])
            c32[0, 0] += dot3(g_real, w_real, NT) - dot3(g_imag, w_imag, NT)
            c32[0, 1] += dot3(g_imag, w_real, NT) + dot3(g_real, w_imag, NT)
            return inner

        lax.fori_loop(0, 4, chunk, 0)
        for ri in range(2):
            r32[ri] = gt[ri, m] + c32[0, ri].reshape(16, 16, 256)

        def to_dest(step, inner):
            dest = 2 * lax.rem(z + 2 + 3 * (step // 2), 4) + lax.rem(step, 2)
            for i in range(2):
                for h in range(2):
                    first = tk[4 * m + 2 * h, 2 * dest + i]
                    second = tk[4 * m + 2 * h + 1, 2 * dest + i]
                    for ri in range(2):
                        rsend[m, dest, i, ri, :, 128 * h : 128 * h + 128] = pick(
                            lambda kb: r32[ri, kb, :, pl.ds(128 * h, 128)], first, second
                        )
            own = jnp.logical_and(dest == k, m == y)

            @pl.when(own)
            def _():
                pltpu.make_async_copy(rsend.at[m, dest], out.at[2 * me + c], r_r.at[2 * me + c]).start()

            @pl.when(jnp.logical_not(own))
            def _():
                r_copy(m, dest, 2 * me + c).start()

            return inner

        lax.fori_loop(0, 8, to_dest, 0)
        return carry

    lax.fori_loop(0, 4, ladder_block, 0)

    for rows in (a_rows, b_rows, w_rows):
        rows.end_near()
        rows.end_other()

    def end_block(m, carry):
        spread_a.end(m)
        spread_w.end(m)

        def end_slot(slot, inner):
            @pl.when(slot != me)
            def _():
                g_copy(m, slot, me).wait_send()

            return inner

        lax.fori_loop(0, 16, end_slot, 0)

        def end_dest(dest, inner):
            @pl.when(jnp.logical_or(dest != k, m != y))
            def _():
                r_copy(m, dest, 2 * me + c).wait_send()

            return inner

        return lax.fori_loop(0, 8, end_dest, carry)

    lax.fori_loop(0, 4, end_block, 0)

    def end_source(source, carry):
        r_copy(0, 0, source).wait_recv()
        return carry

    lax.fori_loop(0, 32, end_source, 0)


def place_kernel(slot_of, parts, out, rows):
    at = 4 * pl.program_id(0)
    lower = lax.broadcasted_iota(jnp.int32, (16, 128), 1) < 64
    for h in range(2):

        def one(kb, carry):
            first, second = slot_of[at + 2 * h, kb], slot_of[at + 2 * h + 1, kb]
            for core in range(2):
                value = jnp.where(
                    lower,
                    parts[2 * first + core, 0, 0, :, pl.ds(128 * h, 128)],
                    parts[2 * second + core, 0, 0, :, pl.ds(128 * h, 128)],
                )
                rows[h, pl.ds(256 * core + kb, 16, stride=16), :] = value
            return carry

        lax.fori_loop(0, 16, one, 0, unroll=True)
        out[0, 0, 128 * h : 128 * h + 128, :] = rows[h].T


def body(amplitudes, integrals, weight, table, transfers, momenta):
    dma = pltpu.SemaphoreType.DMA
    spread_sems = [dma((4,)), dma((4,)), dma((2, 4)), dma((2, 4)), dma((2, 4)), dma((2, 4)), dma((4, 4)), dma((4, 4))]
    parts, slot_of = pl.pallas_call(
        exchange_kernel,
        out_shape=(
            jax.ShapeDtypeStruct((32, 2, 2, 16, 256), F32),
            jax.ShapeDtypeStruct((8, 16), jnp.int32),
        ),
        in_specs=[pl.BlockSpec(memory_space=pl.ANY)] * 6,
        out_specs=(pl.BlockSpec(memory_space=pl.ANY), pl.BlockSpec(memory_space=pltpu.SMEM)),
        scratch_shapes=[
            pltpu.VMEM((2, 4, 4, 256, 512), F32),
            pltpu.VMEM((4, 2, 512, 256), F32),
            pltpu.VMEM((2, 16, 64, 1024), F32),
            pltpu.VMEM((4, 2, 512, 256), BF16),
            pltpu.VMEM((4, 2, 512, 256), BF16),
            pltpu.VMEM((4, 2, 256, 256), F32),
            pltpu.VMEM((2, 2, 256, 128), F32),
            pltpu.VMEM((2, 16, 16, 256), F32),
            pltpu.VMEM((4, 16, 2, 16, 256), F32),
            pltpu.VMEM((4, 16, 2, 16, 256), F32),
            pltpu.VMEM((2, 4, 16, 16, 256), F32),
            pltpu.VMEM((2, 4, 256, 256), BF16),
            pltpu.VMEM((2, 4, 256, 256), BF16),
            pltpu.VMEM((2, 16, 16, 256), F32),
            pltpu.VMEM((4, 8, 2, 2, 16, 256), F32),
            pltpu.SMEM((256, 16), jnp.int32),
            pltpu.SMEM((16,), jnp.int32),
            pltpu.SMEM((16,), jnp.int32),
            pltpu.SMEM((16, 16), jnp.int32),
            pltpu.SMEM((16, 16), jnp.int32),
            pltpu.SMEM((16, 16), jnp.int32),
            pltpu.SMEM((16,), jnp.int32),
            pltpu.SMEM((16,), jnp.int32),
            dma((3,)),
        ]
        + spread_sems
        + spread_sems
        + [dma((4,)), dma((4,)), dma((4, 16)), dma((4, 16)), dma((4, 8)), dma((32,))],
        compiler_params=pltpu.CompilerParams(
            collective_id=0, has_side_effects=True, vmem_limit_bytes=60 * 2**20
        ),
        name="exchange",
    )(amplitudes, integrals, weight, table.reshape(256, 16), transfers, momenta)
    return pl.pallas_call(
        place_kernel,
        grid=(2, 2),
        out_shape=jax.ShapeDtypeStruct((2, 2, 256, 512), F32),
        in_specs=[
            pl.BlockSpec(memory_space=pltpu.SMEM),
            pl.BlockSpec((32, 1, 1, 16, 256), lambda i, ri: (0, i, ri, 0, 0)),
        ],
        out_specs=pl.BlockSpec((1, 1, 256, 512), lambda i, ri: (i, ri, 0, 0)),
        scratch_shapes=[pltpu.VMEM((2, 512, 128), F32)],
        name="place",
    )(slot_of, parts)


def solution(mesh):
    return jax.shard_map(
        body,
        mesh=mesh,
        in_specs=(
            P("kpt", None, "row", "col"),
            P("kpt", None, "row", "col"),
            P("kpt", None, ("row", "col"), None),
            P(),
            P(),
            P(),
        ),
        out_specs=P("kpt", None, "row", "col"),
        check_vma=False,
    )
```

```python
import jax
import jax.numpy as jnp
from jax import lax
from jax.experimental import pallas as pl
from jax.experimental.pallas import tpu as pltpu
from jax.sharding import PartitionSpec as P

MESH = pl.DeviceIdType.MESH
F32 = jnp.float32
BF16 = jnp.bfloat16


def split(value):
    high = value.astype(BF16)
    return high, (value - high.astype(F32)).astype(BF16)


def dot3(left, right, dims):
    def dot(a, b):
        return lax.dot_general(a, b, (dims, ((), ())), preferred_element_type=F32)

    return dot(left[0], right[0]) + (dot(left[0], right[1]) + dot(left[1], right[0]))


def exchange_kernel(
    a_in, b_in, w_in, table_in, transfers_in, momenta_in,
    out, out_table,
    a32, b32, w32, bh, bl, c32, ct, cg, gsend, grecv, gt, gh, gl, r32, rsend,
    table, transfers, momenta, tg, ts, tk, inv_t, inv_m, table_sem,
    a_ys, a_yr, a_xs, a_xr, a_fs, a_fr, a_ss, a_sr,
    w_ys, w_yr, w_xs, w_xr, w_fs, w_fr, w_ss, w_sr,
    b_s, b_r, g_s, g_r, r_s, r_r,
):
    k, y, x = lax.axis_index("kpt"), lax.axis_index("row"), lax.axis_index("col")
    z, c = k // 2, lax.rem(k, 2)
    me = 4 * z + y
    left, right, far = lax.rem(x + 3, 4), lax.rem(x + 1, 4), lax.rem(x + 2, 4)
    right_dev, left_dev, twin = (k, y, right), (k, y, left), (2 * z + 1 - c, y, x)

    def rcopy(src, dst, send_sem, recv_sem, dev):
        return pltpu.make_async_remote_copy(
            src_ref=src, dst_ref=dst, send_sem=send_sem, recv_sem=recv_sem,
            device_id=dev, device_id_type=MESH,
        )

    barrier = pltpu.get_barrier_semaphore()

    for step in range(1, 32):
        dk = 2 * lax.rem(z + step // 8, 4) + lax.rem(c + step // 4 % 2, 2)
        pl.semaphore_signal(
            barrier, inc=1, device_id=(dk, lax.rem(y + step % 4, 4), x), device_id_type=MESH
        )
    pl.semaphore_signal(barrier, inc=1, device_id=right_dev, device_id_type=MESH)
    pl.semaphore_signal(barrier, inc=1, device_id=left_dev, device_id_type=MESH)
    tables = [
        pltpu.make_async_copy(source, dest, table_sem.at[at])
        for at, (source, dest) in enumerate(
            ((table_in, table), (transfers_in, transfers), (momenta_in, momenta))
        )
    ]
    for copy in tables:
        copy.start()
    c32[...] = jnp.zeros_like(c32)
    pl.semaphore_wait(barrier, 33)

    def order(n):
        return lax.rem(y + n + (n // 2) * (1 - 2 * lax.rem(n, 2)), 4)

    def far_order(n):
        return lax.rem(y + 2 + 3 * n + (n // 2) * (3 - 2 * lax.rem(n, 2)), 4)

    near_i, other_i = 1 - lax.rem(y, 2), lax.rem(y, 2)
    home = c == y // 2

    class Rows:
        def __init__(self, source, dest, send, recv):
            self.source, self.dest, self.send, self.recv = source, dest, send, recv

        def copy(self, near, core):
            i = near_i if near else other_i
            return rcopy(
                self.source(i, core), self.dest(core), self.send.at[core if near else 2 + core],
                self.recv.at[y], (2 * z + core, 2 * c + i, x),
            )

        def start_near(self):
            for core in range(2):
                self.copy(True, core).start()

        def start_home(self):
            for core in range(2):

                @pl.when(jnp.logical_and(home, c == core))
                def _():
                    pltpu.make_async_copy(self.source(other_i, core), self.dest(core), self.recv.at[y]).start()

                @pl.when(jnp.logical_and(home, c != core))
                def _():
                    self.copy(False, core).start()

        def start_far(self):
            for core in range(2):

                @pl.when(jnp.logical_not(home))
                def _():
                    self.copy(False, core).start()

        def end_near(self):
            for core in range(2):
                self.copy(True, core).wait_send()

        def end_other(self):
            for core in range(2):

                @pl.when(jnp.logical_not(jnp.logical_and(home, c == core)))
                def _():
                    self.copy(False, core).wait_send()

    class Spread:
        def __init__(self, block, rows, sems):
            self.block, self.rows = block, rows
            self.ys, self.yr, self.xs, self.xr, self.fs, self.fr, self.ss, self.sr = sems

        def wait_row(self, m):
            blk = self.block(c, m, x)
            rcopy(blk, blk, self.ys.at[0], self.yr.at[m], twin).wait_recv()

        def across(self, pos, m):
            at = (x, left, right, far)[pos]
            blk = self.block(c, m, at)
            return rcopy(blk, blk, self.ss.at[pos, m], self.sr.at[pos, m], twin)

        def wait_across(self, m):
            for pos, at in enumerate((x, left, right, far)):
                blk = self.block(1 - c, m, at)
                rcopy(blk, blk, self.ss.at[pos, m], self.sr.at[pos, m], twin).wait_recv()

        def step(self, side, m):
            blk = self.block(c, m, x)
            dev = right_dev if side == 0 else left_dev
            return rcopy(blk, blk, self.xs.at[side, m], self.xr.at[side, m], dev)

        def relay(self, side, m):
            blk = self.half(m, left if side == 0 else right, side)
            dev = right_dev if side == 0 else left_dev
            return rcopy(blk, blk, self.fs.at[side, m], self.fr.at[side, m], dev)

        def half(self, m, at, side):
            return self.block(c, m, at).at[pl.ds(side * (self.rows // 2), self.rows // 2)]

        def forward_own(self, m):
            self.step(0, m).start()
            self.step(1, m).start()
            self.across(0, m).start()

        def forward_near(self, m):
            for side, at in ((0, left), (1, right)):
                blk = self.block(c, m, at)
                rcopy(blk, blk, self.xs.at[side, m], self.xr.at[side, m], twin).wait_recv()
                self.relay(side, m).start()
                self.across(1 + side, m).start()

        def forward_far(self, m):
            for side in range(2):
                blk = self.half(m, far, side)
                rcopy(blk, blk, self.fs.at[side, m], self.fr.at[side, m], twin).wait_recv()
            self.across(3, m).start()

        def end(self, m):
            for side in range(2):
                self.step(side, m).wait_send()
                self.relay(side, m).wait_send()
            for pos in range(4):
                self.across(pos, m).wait_send()

    spread_a = Spread(
        lambda core, m, at: a32.at[core, m, at], 256, (a_ys, a_yr, a_xs, a_xr, a_fs, a_fr, a_ss, a_sr)
    )
    spread_w = Spread(
        lambda core, m, at: w32.at[core, 4 * m + at], 64, (w_ys, w_yr, w_xs, w_xr, w_fs, w_fr, w_ss, w_sr)
    )

    a_rows = Rows(lambda i, core: a_in.at[i, core], lambda core: a32.at[core, y, x], a_ys, a_yr)
    w_rows = Rows(lambda i, core: w_in.at[i, core], lambda core: w32.at[core, 4 * y + x], w_ys, w_yr)
    b_rows = Rows(lambda i, core: b_in.at[i, :, :, pl.ds(256 * core, 256)], lambda core: b32.at[y], b_s, b_r)
    for rows in (a_rows, b_rows, w_rows):
        rows.start_home()
    a_rows.start_near()
    a_rows.start_far()
    b_rows.start_near()
    w_rows.start_near()
    w_rows.start_far()
    b_rows.start_far()
    spread_a.wait_row(y)
    spread_a.forward_own(y)

    for copy in tables:
        copy.wait()

    def add(first, second):
        return table[16 * first + second, 0]

    def sub(first, second):
        return table[16 * first, second]

    def invert(label, carry):
        at_t, at_m = 0, 0
        for slot in range(16):
            at_t = jnp.where(transfers[slot] == label, slot, at_t)
            at_m = jnp.where(momenta[slot] == label, slot, at_m)
        inv_t[label] = at_t
        inv_m[label] = at_m
        return carry

    lax.fori_loop(0, 16, invert, 0)
    own_transfer, own_momentum = transfers[me], momenta[me]

    def fill(ki, carry):
        def one(at, inner):
            tg[ki, at] = sub(sub(momenta[at], own_transfer), ki)
            tk[ki, at] = sub(sub(own_momentum, transfers[at]), ki)
            ts[ki, at] = inv_t[sub(sub(own_momentum, ki), at)]
            return inner

        return lax.fori_loop(0, 16, one, carry)

    lax.fori_loop(0, 16, fill, 0)

    def fill_out(at, carry):
        total = add(transfers[2 * k + at // 4], 4 * y + lax.rem(at, 4))

        def one(kb, inner):
            out_table[at, kb] = inv_m[add(total, kb)]
            return inner

        return lax.fori_loop(0, 16, one, carry)

    lax.fori_loop(0, 8, fill_out, 0)

    def split_b(n):
        at = order(n)
        rcopy(b32.at[at], b32.at[at], b_s.at[0], b_r.at[at], twin).wait_recv()

        def one(ri, carry):
            bh[at, ri], bl[at, ri] = split(b32[at, ri])
            return carry

        lax.fori_loop(0, 2, one, 0)

    NN = ((1,), (0,))
    NT = ((1,), (1,))

    def cycle_chunk(m, at):
        a_real, a_imag = split(a32[0, m, at]), split(a32[1, m, at])
        b_real, b_imag = (bh[at, 0], bl[at, 0]), (bh[at, 1], bl[at, 1])
        c32[m, 0] += dot3(a_real, b_real, NN) - dot3(a_imag, b_imag, NN)
        c32[m, 1] += dot3(a_real, b_imag, NN) + dot3(a_imag, b_real, NN)

    def early_chunks(n):
        m = order(n)
        spread_a.wait_across(m)

        def one(at, carry):
            cycle_chunk(m, order(at))
            return carry

        lax.fori_loop(0, 3, one, 0)

    for n in (1, 2, 3):
        spread_a.wait_row(order(n))
        spread_a.forward_own(order(n))
        if n < 3:
            spread_a.forward_near(order(n - 1))
    split_b(0)
    spread_a.forward_far(y)
    spread_a.forward_near(order(2))
    spread_a.forward_far(order(1))
    spread_a.forward_near(order(3))
    split_b(1)
    split_b(2)
    early_chunks(0)
    spread_a.forward_far(order(2))
    early_chunks(1)
    spread_a.forward_far(order(3))
    for n in range(4):
        spread_w.wait_row(far_order(n))
        spread_w.forward_own(far_order(n))
    early_chunks(2)
    early_chunks(3)
    split_b(3)

    lower = lax.broadcasted_iota(jnp.int32, (16, 128), 1) < 64

    def pick(load, first, second):
        return jnp.where(lower, load(first), load(second))

    def g_copy(m, slot, source):
        return rcopy(
            gsend.at[m, slot], grecv.at[m, source], g_s.at[m, slot], g_r.at[m, source],
            (2 * (slot // 4) + c, lax.rem(slot, 4), x),
        )

    def cycle_block(n, carry):
        m = order(n)
        cycle_chunk(m, order(3))
        for ri in range(2):
            for h in range(2):
                ct[ri, h] = c32[m, ri, 128 * h : 128 * h + 128, :].T
                for kb in range(16):
                    cg[ri, kb, :, 128 * h : 128 * h + 128] = ct[ri, h, pl.ds(kb, 16, stride=16), :]

        def to_slot(step, inner):
            slot_z, slot_y = lax.rem(z + 2 + 3 * (step // 4), 4), lax.rem(y + 2 + 3 * lax.rem(step, 4), 4)
            slot = 4 * slot_z + slot_y
            for h in range(2):
                first, second = tg[4 * m + 2 * h, slot], tg[4 * m + 2 * h + 1, slot]
                for ri in range(2):
                    gsend[m, slot, ri, :, 128 * h : 128 * h + 128] = pick(
                        lambda kb: cg[ri, kb, :, pl.ds(128 * h, 128)], first, second
                    )

            @pl.when(slot == me)
            def _():
                pltpu.make_async_copy(gsend.at[m, slot], grecv.at[m, me], g_r.at[m, me]).start()

            @pl.when(slot != me)
            def _():
                g_copy(m, slot, me).start()

            return inner

        lax.fori_loop(0, 16, to_slot, 0)
        return carry

    lax.fori_loop(0, 4, cycle_block, 0)
    for n in range(4):
        spread_w.forward_near(far_order(n))
    for n in (0, 1):
        spread_w.forward_far(far_order(n))

    def arrive(at, carry):
        slot = at // 4
        g_copy(lax.rem(at, 4), slot, slot).wait_recv()
        return carry

    lax.fori_loop(0, 64, arrive, 0)

    def gather_block(n, carry):
        m = order(n)

        def from_slot(kb, inner):
            for h in range(2):
                first, second = ts[4 * m + 2 * h, kb], ts[4 * m + 2 * h + 1, kb]
                for ri in range(2):
                    gt[ri, m, kb, :, 128 * h : 128 * h + 128] = pick(
                        lambda slot: grecv[m, slot, ri, :, pl.ds(128 * h, 128)], first, second
                    )
            return inner

        lax.fori_loop(0, 16, from_slot, 0)
        for ri in range(2):
            gh[ri, m], gl[ri, m] = split(gt[ri, m].reshape(256, 256))
        return carry

    lax.fori_loop(0, 4, gather_block, 0)

    def r_copy(m, dest, source):
        return rcopy(rsend.at[m, dest], out.at[source], r_s.at[m, dest], r_r.at[source], (dest, m, x))

    def ladder_block(n, carry):
        m = far_order(n)

        @pl.when(n < 2)
        def _():
            spread_w.forward_far(far_order(n + 2))

        spread_w.wait_across(m)
        c32[0] = jnp.zeros_like(c32[0])

        def chunk(at, inner):
            cols = pl.ds(pl.multiple_of(256 * at, 256), 256)
            w_real = split(w32[0, pl.ds(4 * m, 4), :, cols].reshape(256, 256))
            w_imag = split(w32[1, pl.ds(4 * m, 4), :, cols].reshape(256, 256))
            g_real, g_imag = (gh[0, at], gl[0, at]), (gh[1, at], gl[1, at])
            c32[0, 0] += dot3(g_real, w_real, NT) - dot3(g_imag, w_imag, NT)
            c32[0, 1] += dot3(g_imag, w_real, NT) + dot3(g_real, w_imag, NT)
            return inner

        lax.fori_loop(0, 4, chunk, 0)
        for ri in range(2):
            r32[ri] = gt[ri, m] + c32[0, ri].reshape(16, 16, 256)

        def to_dest(step, inner):
            dest = 2 * lax.rem(z + 2 + 3 * (step // 2), 4) + lax.rem(step, 2)
            for i in range(2):
                for h in range(2):
                    first = tk[4 * m + 2 * h, 2 * dest + i]
                    second = tk[4 * m + 2 * h + 1, 2 * dest + i]
                    for ri in range(2):
                        rsend[m, dest, i, ri, :, 128 * h : 128 * h + 128] = pick(
                            lambda kb: r32[ri, kb, :, pl.ds(128 * h, 128)], first, second
                        )
            own = jnp.logical_and(dest == k, m == y)

            @pl.when(own)
            def _():
                pltpu.make_async_copy(rsend.at[m, dest], out.at[2 * me + c], r_r.at[2 * me + c]).start()

            @pl.when(jnp.logical_not(own))
            def _():
                r_copy(m, dest, 2 * me + c).start()

            return inner

        lax.fori_loop(0, 8, to_dest, 0)
        return carry

    lax.fori_loop(0, 4, ladder_block, 0)

    for rows in (a_rows, b_rows, w_rows):
        rows.end_near()
        rows.end_other()

    def end_block(m, carry):
        spread_a.end(m)
        spread_w.end(m)

        def end_slot(slot, inner):
            @pl.when(slot != me)
            def _():
                g_copy(m, slot, me).wait_send()

            return inner

        lax.fori_loop(0, 16, end_slot, 0)

        def end_dest(dest, inner):
            @pl.when(jnp.logical_or(dest != k, m != y))
            def _():
                r_copy(m, dest, 2 * me + c).wait_send()

            return inner

        return lax.fori_loop(0, 8, end_dest, carry)

    lax.fori_loop(0, 4, end_block, 0)

    def end_source(source, carry):
        r_copy(0, 0, source).wait_recv()
        return carry

    lax.fori_loop(0, 32, end_source, 0)


def place_kernel(slot_of, parts, out, rows):
    at = 4 * pl.program_id(0)
    lower = lax.broadcasted_iota(jnp.int32, (16, 128), 1) < 64
    for h in range(2):
        for kb in range(16):
            first, second = slot_of[at + 2 * h, kb], slot_of[at + 2 * h + 1, kb]
            for ri in range(2):
                for core in range(2):
                    value = jnp.where(
                        lower,
                        parts[2 * first + core, 0, ri, :, pl.ds(128 * h, 128)],
                        parts[2 * second + core, 0, ri, :, pl.ds(128 * h, 128)],
                    )
                    rows[ri, h, pl.ds(256 * core + kb, 16, stride=16), :] = value
    for ri in range(2):
        for h in range(2):
            out[0, ri, 128 * h : 128 * h + 128, :] = rows[ri, h].T


def body(amplitudes, integrals, weight, table, transfers, momenta):
    dma = pltpu.SemaphoreType.DMA
    spread_sems = [dma((4,)), dma((4,)), dma((2, 4)), dma((2, 4)), dma((2, 4)), dma((2, 4)), dma((4, 4)), dma((4, 4))]
    parts, slot_of = pl.pallas_call(
        exchange_kernel,
        out_shape=(
            jax.ShapeDtypeStruct((32, 2, 2, 16, 256), F32),
            jax.ShapeDtypeStruct((8, 16), jnp.int32),
        ),
        in_specs=[pl.BlockSpec(memory_space=pl.ANY)] * 6,
        out_specs=(pl.BlockSpec(memory_space=pl.ANY), pl.BlockSpec(memory_space=pltpu.SMEM)),
        scratch_shapes=[
            pltpu.VMEM((2, 4, 4, 256, 512), F32),
            pltpu.VMEM((4, 2, 512, 256), F32),
            pltpu.VMEM((2, 16, 64, 1024), F32),
            pltpu.VMEM((4, 2, 512, 256), BF16),
            pltpu.VMEM((4, 2, 512, 256), BF16),
            pltpu.VMEM((4, 2, 256, 256), F32),
            pltpu.VMEM((2, 2, 256, 128), F32),
            pltpu.VMEM((2, 16, 16, 256), F32),
            pltpu.VMEM((4, 16, 2, 16, 256), F32),
            pltpu.VMEM((4, 16, 2, 16, 256), F32),
            pltpu.VMEM((2, 4, 16, 16, 256), F32),
            pltpu.VMEM((2, 4, 256, 256), BF16),
            pltpu.VMEM((2, 4, 256, 256), BF16),
            pltpu.VMEM((2, 16, 16, 256), F32),
            pltpu.VMEM((4, 8, 2, 2, 16, 256), F32),
            pltpu.SMEM((256, 16), jnp.int32),
            pltpu.SMEM((16,), jnp.int32),
            pltpu.SMEM((16,), jnp.int32),
            pltpu.SMEM((16, 16), jnp.int32),
            pltpu.SMEM((16, 16), jnp.int32),
            pltpu.SMEM((16, 16), jnp.int32),
            pltpu.SMEM((16,), jnp.int32),
            pltpu.SMEM((16,), jnp.int32),
            dma((3,)),
        ]
        + spread_sems
        + spread_sems
        + [dma((4,)), dma((4,)), dma((4, 16)), dma((4, 16)), dma((4, 8)), dma((32,))],
        compiler_params=pltpu.CompilerParams(
            collective_id=0, has_side_effects=True, vmem_limit_bytes=60 * 2**20
        ),
        name="exchange",
    )(amplitudes, integrals, weight, table.reshape(256, 16), transfers, momenta)
    return pl.pallas_call(
        place_kernel,
        grid=(2,),
        out_shape=jax.ShapeDtypeStruct((2, 2, 256, 512), F32),
        in_specs=[
            pl.BlockSpec(memory_space=pltpu.SMEM),
            pl.BlockSpec((32, 1, 2, 16, 256), lambda i: (0, i, 0, 0, 0)),
        ],
        out_specs=pl.BlockSpec((1, 2, 256, 512), lambda i: (i, 0, 0, 0)),
        scratch_shapes=[pltpu.VMEM((2, 2, 512, 128), F32)],
        name="place",
    )(slot_of, parts)


def solution(mesh):
    return jax.shard_map(
        body,
        mesh=mesh,
        in_specs=(
            P("kpt", None, "row", "col"),
            P("kpt", None, "row", "col"),
            P("kpt", None, ("row", "col"), None),
            P(),
            P(),
            P(),
        ),
        out_specs=P("kpt", None, "row", "col"),
        check_vma=False,
    )
```

```python
import jax
import jax.numpy as jnp
from jax import lax
from jax.experimental import pallas as pl
from jax.experimental.pallas import tpu as pltpu
from jax.sharding import PartitionSpec as P

MESH = pl.DeviceIdType.MESH
F32 = jnp.float32
BF16 = jnp.bfloat16


def split(value):
    high = value.astype(BF16)
    return high, (value - high.astype(F32)).astype(BF16)


def dot3(left, right, dims):
    def dot(a, b):
        return lax.dot_general(a, b, (dims, ((), ())), preferred_element_type=F32)

    return dot(left[0], right[0]) + (dot(left[0], right[1]) + dot(left[1], right[0]))


def exchange_kernel(
    a_in, b_in, w_in, table_in, transfers_in, momenta_in,
    out, out_table,
    a32, b32, w32, bh, bl, c32, ct, cg, gsend, grecv, gt, gh, gl, r32, rsend,
    table, transfers, momenta, tg, ts, tk, inv_t, inv_m, table_sem,
    a_ys, a_yr, a_xs, a_xr, a_fs, a_fr, a_ss, a_sr,
    w_ys, w_yr, w_xs, w_xr, w_fs, w_fr, w_ss, w_sr,
    b_s, b_r, g_s, g_r, r_s, r_r,
):
    k, y, x = lax.axis_index("kpt"), lax.axis_index("row"), lax.axis_index("col")
    z, c = k // 2, lax.rem(k, 2)
    me = 4 * z + y
    left, right, far = lax.rem(x + 3, 4), lax.rem(x + 1, 4), lax.rem(x + 2, 4)
    right_dev, left_dev, twin = (k, y, right), (k, y, left), (2 * z + 1 - c, y, x)

    def rcopy(src, dst, send_sem, recv_sem, dev):
        return pltpu.make_async_remote_copy(
            src_ref=src, dst_ref=dst, send_sem=send_sem, recv_sem=recv_sem,
            device_id=dev, device_id_type=MESH,
        )

    barrier = pltpu.get_barrier_semaphore()

    for step in range(1, 32):
        dk = 2 * lax.rem(z + step // 8, 4) + lax.rem(c + step // 4 % 2, 2)
        pl.semaphore_signal(
            barrier, inc=1, device_id=(dk, lax.rem(y + step % 4, 4), x), device_id_type=MESH
        )
    pl.semaphore_signal(barrier, inc=1, device_id=right_dev, device_id_type=MESH)
    pl.semaphore_signal(barrier, inc=1, device_id=left_dev, device_id_type=MESH)
    pl.semaphore_wait(barrier, 33)

    def order(n):
        return lax.rem(y + n + (n // 2) * (1 - 2 * lax.rem(n, 2)), 4)

    def far_order(n):
        return lax.rem(y + 2 + 3 * n, 4)

    near_i, other_i = 1 - lax.rem(y, 2), lax.rem(y, 2)
    home = c == y // 2

    class Rows:
        def __init__(self, source, dest, send, recv):
            self.source, self.dest, self.send, self.recv = source, dest, send, recv

        def copy(self, near, core):
            i = near_i if near else other_i
            return rcopy(
                self.source(i, core), self.dest(core), self.send.at[core if near else 2 + core],
                self.recv.at[y], (2 * z + core, 2 * c + i, x),
            )

        def start_near(self):
            for core in range(2):
                self.copy(True, core).start()

        def start_home(self):
            for core in range(2):

                @pl.when(jnp.logical_and(home, c == core))
                def _():
                    pltpu.make_async_copy(self.source(other_i, core), self.dest(core), self.recv.at[y]).start()

                @pl.when(jnp.logical_and(home, c != core))
                def _():
                    self.copy(False, core).start()

        def start_far(self):
            for core in range(2):

                @pl.when(jnp.logical_not(home))
                def _():
                    self.copy(False, core).start()

        def end_near(self):
            for core in range(2):
                self.copy(True, core).wait_send()

        def end_other(self):
            for core in range(2):

                @pl.when(jnp.logical_not(jnp.logical_and(home, c == core)))
                def _():
                    self.copy(False, core).wait_send()

    class Spread:
        def __init__(self, block, rows, sems):
            self.block, self.rows = block, rows
            self.ys, self.yr, self.xs, self.xr, self.fs, self.fr, self.ss, self.sr = sems

        def wait_row(self, m):
            blk = self.block(c, m, x)
            rcopy(blk, blk, self.ys.at[0], self.yr.at[m], twin).wait_recv()

        def across(self, pos, m):
            at = (x, left, right, far)[pos]
            blk = self.block(c, m, at)
            return rcopy(blk, blk, self.ss.at[pos, m], self.sr.at[pos, m], twin)

        def wait_across(self, m):
            for pos, at in enumerate((x, left, right, far)):
                blk = self.block(1 - c, m, at)
                rcopy(blk, blk, self.ss.at[pos, m], self.sr.at[pos, m], twin).wait_recv()

        def step(self, side, m):
            blk = self.block(c, m, x)
            dev = right_dev if side == 0 else left_dev
            return rcopy(blk, blk, self.xs.at[side, m], self.xr.at[side, m], dev)

        def relay(self, side, m):
            blk = self.half(m, left if side == 0 else right, side)
            dev = right_dev if side == 0 else left_dev
            return rcopy(blk, blk, self.fs.at[side, m], self.fr.at[side, m], dev)

        def half(self, m, at, side):
            return self.block(c, m, at).at[pl.ds(side * (self.rows // 2), self.rows // 2)]

        def forward_own(self, m):
            self.step(0, m).start()
            self.step(1, m).start()
            self.across(0, m).start()

        def forward_near(self, m):
            for side, at in ((0, left), (1, right)):
                blk = self.block(c, m, at)
                rcopy(blk, blk, self.xs.at[side, m], self.xr.at[side, m], twin).wait_recv()
                self.relay(side, m).start()
                self.across(1 + side, m).start()

        def forward_far(self, m):
            for side in range(2):
                blk = self.half(m, far, side)
                rcopy(blk, blk, self.fs.at[side, m], self.fr.at[side, m], twin).wait_recv()
            self.across(3, m).start()

        def end(self, m):
            for side in range(2):
                self.step(side, m).wait_send()
                self.relay(side, m).wait_send()
            for pos in range(4):
                self.across(pos, m).wait_send()

    spread_a = Spread(
        lambda core, m, at: a32.at[core, m, at], 256, (a_ys, a_yr, a_xs, a_xr, a_fs, a_fr, a_ss, a_sr)
    )
    spread_w = Spread(
        lambda core, m, at: w32.at[core, 4 * m + at], 64, (w_ys, w_yr, w_xs, w_xr, w_fs, w_fr, w_ss, w_sr)
    )

    a_rows = Rows(lambda i, core: a_in.at[i, core], lambda core: a32.at[core, y, x], a_ys, a_yr)
    w_rows = Rows(lambda i, core: w_in.at[i, core], lambda core: w32.at[core, 4 * y + x], w_ys, w_yr)
    b_rows = Rows(lambda i, core: b_in.at[i, :, :, pl.ds(256 * core, 256)], lambda core: b32.at[y], b_s, b_r)
    for rows in (a_rows, b_rows, w_rows):
        rows.start_home()
    a_rows.start_near()
    a_rows.start_far()
    b_rows.start_near()
    w_rows.start_near()
    w_rows.start_far()
    b_rows.start_far()
    spread_a.wait_row(y)
    spread_a.forward_own(y)

    tables = [
        pltpu.make_async_copy(source, dest, table_sem.at[at])
        for at, (source, dest) in enumerate(
            ((table_in, table), (transfers_in, transfers), (momenta_in, momenta))
        )
    ]
    for copy in tables:
        copy.start()
    for copy in tables:
        copy.wait()

    def add(first, second):
        return table[16 * first + second, 0]

    def sub(first, second):
        return table[16 * first, second]

    def invert(label, carry):
        at_t, at_m = 0, 0
        for slot in range(16):
            at_t = jnp.where(transfers[slot] == label, slot, at_t)
            at_m = jnp.where(momenta[slot] == label, slot, at_m)
        inv_t[label] = at_t
        inv_m[label] = at_m
        return carry

    lax.fori_loop(0, 16, invert, 0)
    own_transfer, own_momentum = transfers[me], momenta[me]

    def fill(ki, carry):
        def one(at, inner):
            tg[ki, at] = sub(sub(momenta[at], own_transfer), ki)
            tk[ki, at] = sub(sub(own_momentum, transfers[at]), ki)
            ts[ki, at] = inv_t[sub(sub(own_momentum, ki), at)]
            return inner

        return lax.fori_loop(0, 16, one, carry)

    lax.fori_loop(0, 16, fill, 0)

    def fill_out(at, carry):
        total = add(transfers[2 * k + at // 4], 4 * y + lax.rem(at, 4))

        def one(kb, inner):
            out_table[at, kb] = inv_m[add(total, kb)]
            return inner

        return lax.fori_loop(0, 16, one, carry)

    lax.fori_loop(0, 8, fill_out, 0)

    def split_b(n):
        at = order(n)
        rcopy(b32.at[at], b32.at[at], b_s.at[0], b_r.at[at], twin).wait_recv()

        def one(ri, carry):
            bh[at, ri], bl[at, ri] = split(b32[at, ri])
            return carry

        lax.fori_loop(0, 2, one, 0)

    NN = ((1,), (0,))
    NT = ((1,), (1,))

    def cycle_chunk(m, at):
        a_real, a_imag = split(a32[0, m, at]), split(a32[1, m, at])
        b_real, b_imag = (bh[at, 0], bl[at, 0]), (bh[at, 1], bl[at, 1])
        c32[m, 0] += dot3(a_real, b_real, NN) - dot3(a_imag, b_imag, NN)
        c32[m, 1] += dot3(a_real, b_imag, NN) + dot3(a_imag, b_real, NN)

    def early_chunks(n):
        m = order(n)
        spread_a.wait_across(m)

        def one(at, carry):
            cycle_chunk(m, order(at))
            return carry

        lax.fori_loop(0, 3, one, 0)

    c32[...] = jnp.zeros_like(c32)
    for n in (1, 2, 3):
        spread_a.wait_row(order(n))
        spread_a.forward_own(order(n))
        if n < 3:
            spread_a.forward_near(order(n - 1))
    split_b(0)
    spread_a.forward_far(y)
    spread_a.forward_near(order(2))
    spread_a.forward_far(order(1))
    spread_a.forward_near(order(3))
    split_b(1)
    split_b(2)
    early_chunks(0)
    spread_a.forward_far(order(2))
    early_chunks(1)
    spread_a.forward_far(order(3))
    for n in range(4):
        spread_w.wait_row(far_order(n))
        spread_w.forward_own(far_order(n))
    early_chunks(2)
    early_chunks(3)
    split_b(3)

    lower = lax.broadcasted_iota(jnp.int32, (16, 128), 1) < 64

    def pick(load, first, second):
        return jnp.where(lower, load(first), load(second))

    def g_copy(m, slot, source):
        return rcopy(
            gsend.at[m, slot], grecv.at[m, source], g_s.at[m, slot], g_r.at[m, source],
            (2 * (slot // 4) + c, lax.rem(slot, 4), x),
        )

    def cycle_block(n, carry):
        m = order(n)
        cycle_chunk(m, order(3))
        for ri in range(2):
            for h in range(2):
                ct[ri, h] = c32[m, ri, 128 * h : 128 * h + 128, :].T
                for kb in range(16):
                    cg[ri, kb, :, 128 * h : 128 * h + 128] = ct[ri, h, pl.ds(kb, 16, stride=16), :]

        def to_slot(step, inner):
            slot_z, slot_y = lax.rem(z + 2 + 3 * (step // 4), 4), lax.rem(y + 2 + 3 * lax.rem(step, 4), 4)
            slot = 4 * slot_z + slot_y
            for h in range(2):
                first, second = tg[4 * m + 2 * h, slot], tg[4 * m + 2 * h + 1, slot]
                for ri in range(2):
                    gsend[m, slot, ri, :, 128 * h : 128 * h + 128] = pick(
                        lambda kb: cg[ri, kb, :, pl.ds(128 * h, 128)], first, second
                    )

            @pl.when(slot == me)
            def _():
                pltpu.make_async_copy(gsend.at[m, slot], grecv.at[m, me], g_r.at[m, me]).start()

            @pl.when(slot != me)
            def _():
                g_copy(m, slot, me).start()

            return inner

        lax.fori_loop(0, 16, to_slot, 0)
        return carry

    lax.fori_loop(0, 4, cycle_block, 0)
    for n in range(4):
        spread_w.forward_near(far_order(n))
    for n in (0, 1):
        spread_w.forward_far(far_order(n))

    def arrive(at, carry):
        slot = at // 4
        g_copy(lax.rem(at, 4), slot, slot).wait_recv()
        return carry

    lax.fori_loop(0, 64, arrive, 0)

    def gather_block(n, carry):
        m = order(n)

        def from_slot(kb, inner):
            for h in range(2):
                first, second = ts[4 * m + 2 * h, kb], ts[4 * m + 2 * h + 1, kb]
                for ri in range(2):
                    gt[ri, m, kb, :, 128 * h : 128 * h + 128] = pick(
                        lambda slot: grecv[m, slot, ri, :, pl.ds(128 * h, 128)], first, second
                    )
            return inner

        lax.fori_loop(0, 16, from_slot, 0)
        for ri in range(2):
            gh[ri, m], gl[ri, m] = split(gt[ri, m].reshape(256, 256))
        return carry

    lax.fori_loop(0, 4, gather_block, 0)

    def r_copy(m, dest, source):
        return rcopy(rsend.at[m, dest], out.at[source], r_s.at[m, dest], r_r.at[source], (dest, m, x))

    def ladder_block(n, carry):
        m = far_order(n)

        @pl.when(n < 2)
        def _():
            spread_w.forward_far(far_order(n + 2))

        spread_w.wait_across(m)
        c32[0] = jnp.zeros_like(c32[0])

        def chunk(at, inner):
            cols = pl.ds(pl.multiple_of(256 * at, 256), 256)
            w_real = split(w32[0, pl.ds(4 * m, 4), :, cols].reshape(256, 256))
            w_imag = split(w32[1, pl.ds(4 * m, 4), :, cols].reshape(256, 256))
            g_real, g_imag = (gh[0, at], gl[0, at]), (gh[1, at], gl[1, at])
            c32[0, 0] += dot3(g_real, w_real, NT) - dot3(g_imag, w_imag, NT)
            c32[0, 1] += dot3(g_imag, w_real, NT) + dot3(g_real, w_imag, NT)
            return inner

        lax.fori_loop(0, 4, chunk, 0)
        for ri in range(2):
            r32[ri] = gt[ri, m] + c32[0, ri].reshape(16, 16, 256)

        def to_dest(step, inner):
            dest = 2 * lax.rem(z + 2 + 3 * (step // 2), 4) + lax.rem(step, 2)
            for i in range(2):
                for h in range(2):
                    first = tk[4 * m + 2 * h, 2 * dest + i]
                    second = tk[4 * m + 2 * h + 1, 2 * dest + i]
                    for ri in range(2):
                        rsend[m, dest, i, ri, :, 128 * h : 128 * h + 128] = pick(
                            lambda kb: r32[ri, kb, :, pl.ds(128 * h, 128)], first, second
                        )
            own = jnp.logical_and(dest == k, m == y)

            @pl.when(own)
            def _():
                pltpu.make_async_copy(rsend.at[m, dest], out.at[2 * me + c], r_r.at[2 * me + c]).start()

            @pl.when(jnp.logical_not(own))
            def _():
                r_copy(m, dest, 2 * me + c).start()

            return inner

        lax.fori_loop(0, 8, to_dest, 0)
        return carry

    lax.fori_loop(0, 4, ladder_block, 0)

    for rows in (a_rows, b_rows, w_rows):
        rows.end_near()
        rows.end_other()

    def end_block(m, carry):
        spread_a.end(m)
        spread_w.end(m)

        def end_slot(slot, inner):
            @pl.when(slot != me)
            def _():
                g_copy(m, slot, me).wait_send()

            return inner

        lax.fori_loop(0, 16, end_slot, 0)

        def end_dest(dest, inner):
            @pl.when(jnp.logical_or(dest != k, m != y))
            def _():
                r_copy(m, dest, 2 * me + c).wait_send()

            return inner

        return lax.fori_loop(0, 8, end_dest, carry)

    lax.fori_loop(0, 4, end_block, 0)

    def end_source(source, carry):
        r_copy(0, 0, source).wait_recv()
        return carry

    lax.fori_loop(0, 32, end_source, 0)


def place_kernel(slot_of, parts, out, rows):
    at = 4 * pl.program_id(0)
    lower = lax.broadcasted_iota(jnp.int32, (16, 128), 1) < 64
    for h in range(2):
        for kb in range(16):
            first, second = slot_of[at + 2 * h, kb], slot_of[at + 2 * h + 1, kb]
            for ri in range(2):
                for core in range(2):
                    value = jnp.where(
                        lower,
                        parts[2 * first + core, 0, ri, :, pl.ds(128 * h, 128)],
                        parts[2 * second + core, 0, ri, :, pl.ds(128 * h, 128)],
                    )
                    rows[ri, h, pl.ds(256 * core + kb, 16, stride=16), :] = value
    for ri in range(2):
        for h in range(2):
            out[0, ri, 128 * h : 128 * h + 128, :] = rows[ri, h].T


def body(amplitudes, integrals, weight, table, transfers, momenta):
    dma = pltpu.SemaphoreType.DMA
    spread_sems = [dma((4,)), dma((4,)), dma((2, 4)), dma((2, 4)), dma((2, 4)), dma((2, 4)), dma((4, 4)), dma((4, 4))]
    parts, slot_of = pl.pallas_call(
        exchange_kernel,
        out_shape=(
            jax.ShapeDtypeStruct((32, 2, 2, 16, 256), F32),
            jax.ShapeDtypeStruct((8, 16), jnp.int32),
        ),
        in_specs=[pl.BlockSpec(memory_space=pl.ANY)] * 6,
        out_specs=(pl.BlockSpec(memory_space=pl.ANY), pl.BlockSpec(memory_space=pltpu.SMEM)),
        scratch_shapes=[
            pltpu.VMEM((2, 4, 4, 256, 512), F32),
            pltpu.VMEM((4, 2, 512, 256), F32),
            pltpu.VMEM((2, 16, 64, 1024), F32),
            pltpu.VMEM((4, 2, 512, 256), BF16),
            pltpu.VMEM((4, 2, 512, 256), BF16),
            pltpu.VMEM((4, 2, 256, 256), F32),
            pltpu.VMEM((2, 2, 256, 128), F32),
            pltpu.VMEM((2, 16, 16, 256), F32),
            pltpu.VMEM((4, 16, 2, 16, 256), F32),
            pltpu.VMEM((4, 16, 2, 16, 256), F32),
            pltpu.VMEM((2, 4, 16, 16, 256), F32),
            pltpu.VMEM((2, 4, 256, 256), BF16),
            pltpu.VMEM((2, 4, 256, 256), BF16),
            pltpu.VMEM((2, 16, 16, 256), F32),
            pltpu.VMEM((4, 8, 2, 2, 16, 256), F32),
            pltpu.SMEM((256, 16), jnp.int32),
            pltpu.SMEM((16,), jnp.int32),
            pltpu.SMEM((16,), jnp.int32),
            pltpu.SMEM((16, 16), jnp.int32),
            pltpu.SMEM((16, 16), jnp.int32),
            pltpu.SMEM((16, 16), jnp.int32),
            pltpu.SMEM((16,), jnp.int32),
            pltpu.SMEM((16,), jnp.int32),
            dma((3,)),
        ]
        + spread_sems
        + spread_sems
        + [dma((4,)), dma((4,)), dma((4, 16)), dma((4, 16)), dma((4, 8)), dma((32,))],
        compiler_params=pltpu.CompilerParams(
            collective_id=0, has_side_effects=True, vmem_limit_bytes=60 * 2**20
        ),
        name="exchange",
    )(amplitudes, integrals, weight, table.reshape(256, 16), transfers, momenta)
    return pl.pallas_call(
        place_kernel,
        grid=(2,),
        out_shape=jax.ShapeDtypeStruct((2, 2, 256, 512), F32),
        in_specs=[
            pl.BlockSpec(memory_space=pltpu.SMEM),
            pl.BlockSpec((32, 1, 2, 16, 256), lambda i: (0, i, 0, 0, 0)),
        ],
        out_specs=pl.BlockSpec((1, 2, 256, 512), lambda i: (i, 0, 0, 0)),
        scratch_shapes=[pltpu.VMEM((2, 2, 512, 128), F32)],
        name="place",
    )(slot_of, parts)


def solution(mesh):
    return jax.shard_map(
        body,
        mesh=mesh,
        in_specs=(
            P("kpt", None, "row", "col"),
            P("kpt", None, "row", "col"),
            P("kpt", None, ("row", "col"), None),
            P(),
            P(),
            P(),
        ),
        out_specs=P("kpt", None, "row", "col"),
        check_vma=False,
    )
```
